32 devices in a mesh: gx: 4 (over y, core), gy: 8 (over z, x).
Axes of the slice: x: 2, y: 2, z: 4, core: 2. Of those that a mesh axis runs over, the one named last changes fastest.
Arguments:
- perm: float32 [40, 80, 640], P('gx', 'gy'), may hold values from 0.05 to 5
- storage: float32 [40, 80, 640], P('gx', 'gy'), may hold values from 0.2 to 2
- source: float32 [40, 80, 640], P('gx', 'gy'), may hold values from -40 to 40
- weight: float32 [40, 80, 640], P('gx', 'gy'), may hold values from 0.5 to 1.5
- block_map: int32 [40, 80, 640], P('gx', 'gy'), may hold values from 0 to 63, as said below
- coarse_matrix: float32 [27, 4, 8, 64], P(None, 'gx', 'gy'), may hold values from -200 to 2000, as said below
Outputs:
- pressure: float32 [40, 80, 640], P('gx', 'gy')
- final_residual: float32 [40, 80, 640], P('gx', 'gy')
The draws below stay inside these ranges and needn't reach their ends.
Inputs may be any that keep to these rules, and one draw needn't show every extreme that they name: `block_map`: each cell's number l names a coarse block of its own device's brick of 10 x 10 x 640 cells, naming the l-th block of 10 cells along z inside the brick: the block that contains the cell, or, for a cell on the first layer of a block along a dimension that is not the brick's face, possibly the previous block along that dimension. `coarse_matrix`: for every block, entry 13 is positive and larger than the sum of the magnitudes of the other 26 entries; the other entries are zero or negative, zero where the offset leaves the block grid, and entry o at a block equals entry 26 - o at the block shifted by offset o.
All inputs are finite; a program needn't handle non-finite values.
Results may differ from the reference program's by a relative error of at most 0.0003.
Values sent between devices are 32-bit elements; how exact they have to be, the bound alone decides.
A program may use at most 64 MiB of HBM per device.

```python
import math
import jax
import jax.numpy as jnp
from jax import lax

BLOCK = 10
ITERS = 6
CX = 10
CY = 10
NZ = 640
NX = 40
NY = 80
CBX = 1
CBY = 1
CBZ = 64
NCX = 4
NCY = 8


def draw_source(key, part):
    key = jax.random.fold_in(key, 7)
    along_x = lax.broadcasted_iota(jnp.float32, (NX, 1, 1), 0) / NX
    along_y = lax.broadcasted_iota(jnp.float32, (1, NY, 1), 1) / NY
    ramped = (1.0 + 0.8 * along_x) * (1.0 + 0.8 * along_y)
    base = jax.random.truncated_normal(key, -6.0, 6.0, (NX, NY, NZ), jnp.float32)
    return 2.0 * base * ramped


def draw_block_map(key, part):
    key = jax.random.fold_in(key, 11)
    extent = (NX, NY, NZ)
    key_x, key_y, key_z = jax.random.split(key, 3)
    local_x = lax.broadcasted_iota(jnp.int32, extent, 0) % CX
    local_y = lax.broadcasted_iota(jnp.int32, extent, 1) % CY
    local_z = lax.broadcasted_iota(jnp.int32, extent, 2)
    block_x = local_x // BLOCK - jnp.where((local_x % BLOCK == 0) & (local_x > 0), jax.random.randint(key_x, extent, 0, 2), 0)
    block_y = local_y // BLOCK - jnp.where((local_y % BLOCK == 0) & (local_y > 0), jax.random.randint(key_y, extent, 0, 2), 0)
    block_z = local_z // BLOCK - jnp.where((local_z % BLOCK == 0) & (local_z > 0), jax.random.randint(key_z, extent, 0, 2), 0)
    return ((block_x * CBY + block_y) * CBZ + block_z).astype(jnp.int32)


def draw_coarse_matrix(key, part):
    key = jax.random.fold_in(key, 5)
    extent = (NCX, NCY, CBZ)
    key_factor, key_margin = jax.random.split(key, 2)
    factor = jax.random.uniform(key_factor, (27,) + extent, jnp.float32, 0.5, 1.5)
    margin = jax.random.uniform(key_margin, extent, jnp.float32, 0.02, 0.08)
    blocks_x = lax.broadcasted_iota(jnp.int32, extent, 0)
    blocks_y = lax.broadcasted_iota(jnp.int32, extent, 1)
    blocks_z = lax.broadcasted_iota(jnp.int32, extent, 2)
    scales = (0.0, 60.0, 8.0, 2.0)
    inside_list = []
    weights = []
    for offset in range(27):
        delta_x = offset // 9 - 1
        delta_y = offset // 3 % 3 - 1
        delta_z = offset % 3 - 1
        inside = (blocks_x + delta_x >= 0) & (blocks_x + delta_x < NCX) & (blocks_y + delta_y >= 0) & (blocks_y + delta_y < NCY) & (blocks_z + delta_z >= 0) & (blocks_z + delta_z < CBZ)
        inside_list.append(inside)
        weights.append(jnp.where(inside, factor[offset] * scales[abs(delta_x) + abs(delta_y) + abs(delta_z)], 0.0))
    entries = []
    for offset in range(27):
        delta_x = offset // 9 - 1
        delta_y = offset // 3 % 3 - 1
        delta_z = offset % 3 - 1
        padded = jnp.pad(weights[26 - offset], 1)
        moved = padded[1 + delta_x:1 + delta_x + NCX, 1 + delta_y:1 + delta_y + NCY, 1 + delta_z:1 + delta_z + CBZ]
        entries.append(jnp.where(inside_list[offset], -0.5 * (weights[offset] + moved), 0.0))
    summed = jnp.zeros(extent, jnp.float32)
    for offset in range(27):
        if offset != 13:
            summed = summed + jnp.abs(entries[offset])
    entries[13] = (1.0 + margin) * summed
    return jnp.stack(entries).astype(jnp.float32)


def shard_levels(key, dims, shards, low, top_value):
    loudness = 1.0
    for position, parts in shards:
        steps = jax.random.uniform(jax.random.fold_in(jax.random.fold_in(key, 6), position), (parts,), jnp.float32, low / len(shards), top_value / len(shards))
        loudness = loudness * jnp.repeat(jnp.exp(steps), dims[position] // parts).reshape((-1,) + (1,) * (len(dims) - 1 - position))
    return loudness


def setup_inputs(seed: int = 0) -> dict:
    streams_of = jax.random.split(jax.random.key(seed), 7)
    return {
        "perm": jnp.clip(jnp.exp(math.log(5.0) - 4.6051702 * jax.random.uniform(streams_of[0], (NX, NY, NZ), jnp.float32) ** shard_levels(streams_of[0], (NX, NY, NZ), ((0, 4), (1, 8)), -0.2, 0.2)), 0.05, 5.0),
        "storage": jnp.clip(jnp.exp(math.log(2.0) - 2.3025851 * jax.random.uniform(streams_of[1], (NX, NY, NZ), jnp.float32) ** shard_levels(streams_of[1], (NX, NY, NZ), ((0, 4), (1, 8)), -0.2, 0.2)), 0.2, 2.0),
        "source": draw_source(jax.random.fold_in(streams_of[6], 71), 0),
        "weight": jnp.clip(0.5 + 1.0 * jax.random.uniform(streams_of[3], (NX, NY, NZ), jnp.float32) ** shard_levels(streams_of[3], (NX, NY, NZ), ((0, 4), (1, 8)), -0.2, 0.2), 0.5, 1.5),
        "block_map": draw_block_map(jax.random.fold_in(streams_of[6], 71), 0),
        "coarse_matrix": draw_coarse_matrix(jax.random.fold_in(streams_of[6], 71), 0),
    }


OMEGA = 0.8


def harmonic(cell_perm, other_perm):
    return 2.0 * cell_perm * other_perm / (cell_perm + other_perm)


def face_terms(padded):
    center = padded[1:-1, 1:-1, 1:-1]
    return (harmonic(center, padded[2:, 1:-1, 1:-1]), harmonic(center, padded[:-2, 1:-1, 1:-1]),
            harmonic(center, padded[1:-1, 2:, 1:-1]), harmonic(center, padded[1:-1, :-2, 1:-1]),
            harmonic(center, padded[1:-1, 1:-1, 2:]), harmonic(center, padded[1:-1, 1:-1, :-2]))


def diagonal_of(face_list, storage):
    return storage + (((((face_list[0] + face_list[1]) + face_list[2]) + face_list[3]) + face_list[4]) + face_list[5])


def neighbour_flux(face_list, padded):
    summed = face_list[0] * padded[2:, 1:-1, 1:-1] + face_list[1] * padded[:-2, 1:-1, 1:-1]
    summed = summed + face_list[2] * padded[1:-1, 2:, 1:-1] + face_list[3] * padded[1:-1, :-2, 1:-1]
    summed = summed + face_list[4] * padded[1:-1, 1:-1, 2:] + face_list[5] * padded[1:-1, 1:-1, :-2]
    return summed


def coarse_apply(matrix, padded):
    extent = matrix.shape[1:]
    summed = jnp.zeros(extent, jnp.float32)
    for offset in range(27):
        shift_x = offset // 9
        shift_y = offset // 3 % 3
        shift_z = offset % 3
        summed = summed + matrix[offset] * padded[shift_x:shift_x + extent[0], shift_y:shift_y + extent[1], shift_z:shift_z + extent[2]]
    return summed


def conjugate(matrix, coarse_rhs):
    solution = jnp.zeros_like(coarse_rhs)
    residual = coarse_rhs
    direction = coarse_rhs
    norm_now = jnp.sum(residual * residual)
    for iteration in range(ITERS):
        applied = coarse_apply(matrix, jnp.pad(direction, 1))
        step_size = norm_now / jnp.sum(direction * applied)
        solution = solution + step_size * direction
        residual = residual - step_size * applied
        if iteration + 1 < ITERS:
            norm_next = jnp.sum(residual * residual)
            direction = residual + (norm_next / norm_now) * direction
            norm_now = norm_next
    return solution


def reference(perm, storage, source, weight, block_map, coarse_matrix):
    face_list = face_terms(jnp.pad(perm, 1))
    diagonal = diagonal_of(face_list, storage)

    def operate(values):
        return diagonal * values - neighbour_flux(face_list, jnp.pad(values, 1))

    sweep_one = OMEGA * source / diagonal
    second = sweep_one + OMEGA * (source - operate(sweep_one)) / diagonal
    fine_residual = source - operate(second)
    rows_x = lax.broadcasted_iota(jnp.int32, (NX, 1, 1), 0)
    rows_y = lax.broadcasted_iota(jnp.int32, (1, NY, 1), 1)
    global_x = rows_x // CX * CBX + block_map // (CBY * CBZ)
    global_y = rows_y // CY * CBY + block_map // CBZ % CBY
    global_id = ((global_x * NCY + global_y) * CBZ + block_map % CBZ).astype(jnp.int32)
    coarse_rhs = jax.ops.segment_sum((weight * fine_residual).reshape(-1), global_id.reshape(-1),
                                     num_segments=NCX * NCY * CBZ).reshape(NCX, NCY, CBZ)
    correction = conjugate(coarse_matrix, coarse_rhs)
    pressure = second + weight * correction.reshape(-1)[global_id]
    final_residual = source - operate(pressure)
    return pressure, final_residual
```

```python
import functools

import jax
import jax.numpy as jnp
from jax import lax
from jax.experimental import pallas as pl
from jax.experimental.pallas import tpu as pltpu
from jax.sharding import PartitionSpec as P

ITERS = 6
OMEGA = 0.8
MESH = pl.DeviceIdType.MESH
F32 = jnp.float32


def harmonic(a, b):
    return 2.0 * a * b / (a + b)


def pieces(value):
    high = value.astype(jnp.bfloat16).astype(F32)
    rest = value - high
    middle = rest.astype(jnp.bfloat16).astype(F32)
    return high, middle, rest - middle


def kernel(
    ngx, ngy, block,
    perm_h, storage_h, source_h, weight_h, map_h, matrix_h,
    pressure_h, final_h,
    perm_v, storage_v, source_v, weight_v, map_v, matrix_v,
    pad_p, v1, v2, tx, typ, tym, tzp, tzm, diag, inv,
    sy, ry, sx, sym, rym, px, wx, mx,
    tile, gm, coef, row, gr, field, spread, ind, indt,
    pressure_v, final_v,
    local_sem, send_sem, recv_sem, gsend_sem, grecv_sem,
):
    n = ngx * ngy
    cx, cy, nz = perm_v.shape
    blocks = matrix_v.shape[-1]
    gx, gy = lax.axis_index("gx"), lax.axis_index("gy")
    me = gx * ngy + gy
    has = (gy > 0, gy < ngy - 1, gx > 0, gx < ngx - 1)
    near = ((gx, gy - 1), (gx, gy + 1), (gx - 1, gy), (gx + 1, gy))

    loads = [
        pltpu.make_async_copy(src, dst, local_sem.at[i])
        for i, (src, dst) in enumerate((
            (perm_h, perm_v), (matrix_h, matrix_v), (source_h, source_v),
            (storage_h, storage_v), (weight_h, weight_v), (map_h, map_v),
        ))
    ]
    for load in loads:
        load.start()

    def other(k):
        t = lax.rem(me + k, n)
        return (t // ngy, lax.rem(t, ngy))

    barrier = pltpu.get_barrier_semaphore()

    @pl.loop(1, n)
    def _(k):
        pl.semaphore_signal(barrier, inc=1, device_id=other(k), device_id_type=MESH)

    for d in range(2):
        @pl.when(jnp.logical_not(has[d]))
        def _():
            for s in range(4):
                ry[s, d] = jnp.zeros(ry.shape[2:], F32)
            rym[d] = jnp.zeros(rym.shape[1:], jnp.int32)

        @pl.when(jnp.logical_not(has[2 + d]))
        def _():
            px[d] = jnp.zeros(px.shape[1:], F32)
            wx[d] = jnp.zeros(wx.shape[1:], F32)
            mx[d] = jnp.zeros(mx.shape[1:], jnp.int32)
            for v in (v1, v2):
                v[d * (cx + 1)] = jnp.zeros(v.shape[1:], F32)

    zid = lax.broadcasted_iota(jnp.int32, (nz, 128), 0) // block
    ind[...] = (zid == lax.broadcasted_iota(jnp.int32, (nz, 128), 1)).astype(F32).astype(jnp.bfloat16)
    zidt = lax.broadcasted_iota(jnp.int32, (128, nz), 1) // block
    indt[...] = (zidt == lax.broadcasted_iota(jnp.int32, (128, nz), 0)).astype(F32).astype(jnp.bfloat16)
    pad_p[...] = jnp.ones(pad_p.shape, F32)
    tile[...] = jnp.zeros(tile.shape, F32)
    sx[...] = jnp.zeros(sx.shape, F32)

    pl.semaphore_wait(barrier, n - 1)

    def halo(stage, d, src, dst):
        return pltpu.make_async_remote_copy(
            src_ref=src, dst_ref=dst,
            send_sem=send_sem.at[stage * 4 + d],
            recv_sem=recv_sem.at[stage * 4 + (d ^ 1)],
            device_id=near[d], device_id_type=MESH,
        )

    def send(stage, d, src, dst):
        @pl.when(has[d])
        def _():
            halo(stage, d, src, dst).start()

    def wait_sent(stage, d, src, dst):
        @pl.when(has[d])
        def _():
            halo(stage, d, src, dst).wait_send()

    def wait_halo(stage, d, dst):
        @pl.when(has[d])
        def _():
            pltpu.make_async_remote_copy(
                src_ref=dst, dst_ref=dst,
                send_sem=send_sem.at[stage * 4 + d],
                recv_sem=recv_sem.at[stage * 4 + d],
                device_id=near[d], device_id_type=MESH,
            ).wait_recv()

    sent = []

    def go(stage, d, src, dst):
        send(stage, d, src, dst)
        sent.append((stage, d, src, dst))

    for d in range(2):
        go(0, 2 + d, perm_h.at[(cx - 1) * d], px.at[d ^ 1])
    loads[0].wait()

    @pl.loop(0, cx)
    def _(x):
        p = perm_v[x]
        pad_p[x + 1, 0:cy] = p
        sy[0, 0, pl.ds(x, 1)] = p[0:1]
        sy[0, 1, pl.ds(x, 1)] = p[cy - 1 : cy]

    for d in range(2):
        go(0, d, sy.at[0, d], ry.at[0, d ^ 1])

    loads[1].wait()
    for p in range(7):
        tile[p : p + 1, 0:blocks] = matrix_v[p, 0]
        tile[p : p + 1, 64 : 64 + blocks] = matrix_v[p + 7, 0]

    def matrix_copy(k):
        return pltpu.make_async_remote_copy(
            src_ref=tile, dst_ref=gm.at[pl.ds(pl.multiple_of(me * 8, 8), 8)],
            send_sem=gsend_sem.at[0], recv_sem=grecv_sem.at[0],
            device_id=other(k), device_id_type=MESH,
        )

    loads[4].wait()
    loads[5].wait()

    @pl.loop(0, cx)
    def _(x):
        w = weight_v[x]
        sy[3, 0, pl.ds(x, 1)] = w[0:1]
        sy[3, 1, pl.ds(x, 1)] = w[cy - 1 : cy]
        m = map_v[x]
        sym[0, pl.ds(x, 1)] = m[0:1]
        sym[1, pl.ds(x, 1)] = m[cy - 1 : cy]

    loads[2].wait()
    loads[3].wait()

    for d in range(4):
        wait_halo(0, d, ry.at[0, d] if d < 2 else px.at[d - 2])

    def to_rows(buffer, stage):
        @pl.loop(0, cx)
        def _(x):
            buffer[x + 1, 15:16] = ry[stage, 0, pl.ds(x, 1)]
            buffer[x + 1, cy : cy + 1] = ry[stage, 1, pl.ds(x, 1)]

    pad_p[0, 0:cy] = px[0]
    pad_p[cx + 1, 0:cy] = px[1]
    to_rows(pad_p, 0)

    tx[0] = harmonic(pad_p[0], pad_p[1])
    lane = lax.broadcasted_iota(jnp.int32, (16, nz), 1)

    @pl.loop(0, cx)
    def _(x):
        p = pad_p[x + 1]
        up = harmonic(p, pad_p[x + 2])
        tx[x + 1] = up
        yp = harmonic(p, pltpu.roll(p, 15, 0))
        ym = pltpu.roll(yp, 1, 0)
        zp = jnp.where(lane == nz - 1, 0.0, harmonic(p, pltpu.roll(p, nz - 1, 1)))
        zm = pltpu.roll(zp, 1, 1)
        typ[x] = yp[0:cy]
        tym[x] = ym[0:cy]
        tzp[x] = zp[0:cy]
        tzm[x] = zm[0:cy]
        total = storage_v[x] + (up + tx[x] + yp + ym + zp + zm)[0:cy]
        inverse = 1.0 / total
        diag[x] = total
        inv[x] = inverse
        first = OMEGA * source_v[x] * inverse
        v1[x + 1, 0:cy] = first
        sy[1, 0, pl.ds(x, 1)] = first[0:1]
        sy[1, 1, pl.ds(x, 1)] = first[cy - 1 : cy]

    def field_halo(stage, v):
        for d in range(2):
            go(stage, d, sy.at[stage, d], ry.at[stage, d ^ 1])
        for d in range(2):
            sx[stage - 1, d, 0:cy] = v[1 + (cx - 1) * d, 0:cy]
            go(stage, 2 + d, sx.at[stage - 1, d], v.at[(cx + 1) * (1 - d)])

    def field_wait(stage, v):
        for d in range(4):
            wait_halo(stage, d, ry.at[stage, d] if d < 2 else v.at[(cx + 1) * (d - 2)])

    def operate(v, x):
        c = v[x + 1]
        total = tx[x + 1, 0:cy] * v[x + 2, 0:cy] + tx[x, 0:cy] * v[x, 0:cy]
        total += typ[x] * pltpu.roll(c, 15, 0)[0:cy] + tym[x] * pltpu.roll(c, 1, 0)[0:cy]
        total += tzp[x] * pltpu.roll(c, nz - 1, 1)[0:cy] + tzm[x] * pltpu.roll(c, 1, 1)[0:cy]
        return c[0:cy], diag[x] * c[0:cy] - total

    field_halo(1, v1)

    @pl.loop(1, n)
    def _(k):
        matrix_copy(k).start()

    gm[pl.ds(pl.multiple_of(me * 8, 8), 8)] = tile[...]

    field_wait(1, v1)
    to_rows(v1, 1)

    @pl.loop(0, cx)
    def _(x):
        c, image = operate(v1, x)
        second = c + OMEGA * (source_v[x] - image) * inv[x]
        v2[x + 1, 0:cy] = second
        sy[2, 0, pl.ds(x, 1)] = second[0:1]
        sy[2, 1, pl.ds(x, 1)] = second[cy - 1 : cy]

    field_halo(2, v2)

    for d in range(2):
        go(3, d, sy.at[3, d], ry.at[3, d ^ 1])
        go(4, d, sym.at[d], rym.at[d ^ 1])
        go(3, 2 + d, weight_h.at[(cx - 1) * d], wx.at[d ^ 1])
        go(4, 2 + d, map_h.at[(cx - 1) * d], mx.at[d ^ 1])

    field_wait(2, v2)
    to_rows(v2, 2)

    zblock = lax.broadcasted_iota(jnp.int32, (cy, nz), 1) // block

    def gather(x, carry):
        same, before = carry
        c, image = operate(v2, x)
        value = weight_v[x] * (source_v[x] - image)
        here = map_v[x] == zblock
        return same + jnp.where(here, value, 0.0), before + jnp.where(here, 0.0, value)

    zero = jnp.zeros((cy, nz), F32)
    same, before = lax.fori_loop(0, cx, gather, (zero, zero))
    same = jnp.broadcast_to(jnp.sum(same, axis=0, keepdims=True), (16, nz))
    before = jnp.broadcast_to(jnp.sum(before, axis=0, keepdims=True), (16, nz))
    high, middle, low = pieces(same + pltpu.roll(before, nz - 1, 1))
    rows = lax.broadcasted_iota(jnp.int32, (16, nz), 0)
    stacked = jnp.where(rows == 0, high, jnp.where(rows == 1, middle, jnp.where(rows == 2, low, 0.0)))
    sums = jnp.dot(stacked.astype(jnp.bfloat16), ind[...], preferred_element_type=F32)
    mine = jnp.sum(sums, axis=0, keepdims=True)
    row[...] = mine

    def row_copy(k):
        return pltpu.make_async_remote_copy(
            src_ref=row, dst_ref=gr.at[me],
            send_sem=gsend_sem.at[1], recv_sem=grecv_sem.at[1],
            device_id=other(k), device_id_type=MESH,
        )

    @pl.loop(1, n)
    def _(k):
        row_copy(k).start()

    gr[me] = mine

    def all_of(buffer, size, which):
        part = buffer.at[pl.ds(0, size)]
        return pltpu.make_async_remote_copy(
            src_ref=part, dst_ref=part,
            send_sem=gsend_sem.at[which], recv_sem=grecv_sem.at[which],
            device_id=other(1), device_id_type=MESH,
        )

    all_of(gm, (n - 1) * 8, 0).wait_recv()
    lower = lax.broadcasted_iota(jnp.int32, (ngy, 128), 1) < 64
    for p in range(7):
        for g in range(ngx):
            both = gm[pl.ds(g * ngy * 8 + p, ngy, stride=8), :]
            coef[p, g] = jnp.where(lower, both, 0.0)
            coef[p + 7, g] = jnp.where(lower, pltpu.roll(both, 64, 1), 0.0)

    def moved(plane, dy, dz):
        if dz:
            plane = pltpu.roll(plane, dz % 128, 1)
        if dy:
            plane = pltpu.roll(plane, dy % ngy, 0)
        return plane

    for o in range(13):
        dx, dy, dz = o // 9 - 1, o // 3 % 3 - 1, o % 3 - 1
        for g in range(ngx):
            coef[26 - o, g] = moved(coef[o, (g - dx) % ngx], dy, dz)

    all_of(gr, n - 1, 1).wait_recv()
    for g in range(ngx):
        for h in range(ngy):
            field[g, h : h + 1] = gr[g * ngy + h]

    def apply(u):
        result = [None] * ngx
        for dy in (-1, 0, 1):
            for dz in (-1, 0, 1):
                shifted = [moved(plane, -dy, -dz) for plane in u]
                for dx in (-1, 0, 1):
                    o = 9 * (dx + 1) + 3 * (dy + 1) + dz + 1
                    for g in range(ngx):
                        if 0 <= g + dx < ngx:
                            term = coef[o, g] * shifted[g + dx]
                            result[g] = term if result[g] is None else result[g] + term
        return result

    def inner(a, b):
        total = a[0] * b[0]
        for g in range(1, ngx):
            total = total + a[g] * b[g]
        return jnp.sum(jnp.sum(total, axis=0, keepdims=True), axis=1, keepdims=True)

    residual = [field[g] for g in range(ngx)]
    direction = residual
    answer = [jnp.zeros((ngy, 128), F32)] * ngx
    norm = inner(residual, residual)
    for iteration in range(ITERS):
        applied = apply(direction)
        step = norm / inner(direction, applied)
        answer = [a + step * b for a, b in zip(answer, direction)]
        if iteration + 1 < ITERS:
            residual = [a - step * b for a, b in zip(residual, applied)]
            following = inner(residual, residual)
            ratio = following / norm
            direction = [a + ratio * b for a, b in zip(residual, direction)]
            norm = following
    for g in range(ngx):
        field[g] = answer[g]

    west, east = jnp.maximum(gx - 1, 0), jnp.minimum(gx + 1, ngx - 1)
    south, north = jnp.maximum(gy - 1, 0), jnp.minimum(gy + 1, ngy - 1)
    picks = ((gx, gy), (gx, south), (gx, north), (west, gy), (east, gy))
    rows = lax.broadcasted_iota(jnp.int32, (16, 128), 0)
    stacked = jnp.zeros((16, 128), F32)
    for i, (a, b) in enumerate(picks):
        value = jnp.broadcast_to(field[a, pl.ds(b, 1)], (16, 128))
        for j, piece in enumerate(pieces(value)):
            stacked = jnp.where(rows == 3 * i + j, piece, stacked)
    spread[...] = jnp.dot(stacked.astype(jnp.bfloat16), indt[...], preferred_element_type=F32)

    def by_block(i):
        value = spread[3 * i : 3 * i + 1] + spread[3 * i + 1 : 3 * i + 2] + spread[3 * i + 2 : 3 * i + 3]
        value = jnp.broadcast_to(value, (16, nz))
        return value[0:cy], pltpu.roll(value, 1, 1)[0:cy]

    for d in range(4):
        wait_halo(3, d, ry.at[3, d] if d < 2 else wx.at[d - 2])
        wait_halo(4, d, rym.at[d] if d < 2 else mx.at[d - 2])

    for d in range(2):
        now, prior = by_block(1 + d)
        ry[2, d] = ry[2, d] + ry[3, d] * jnp.where(rym[d] == zblock, now, prior)
        now, prior = by_block(3 + d)
        at = d * (cx + 1)
        v1[at, 0:cy] = v2[at, 0:cy] + wx[d] * jnp.where(mx[d] == zblock, now, prior)

    now, prior = by_block(0)

    @pl.loop(0, cx)
    def _(x):
        value = v2[x + 1, 0:cy] + weight_v[x] * jnp.where(map_v[x] == zblock, now, prior)
        pressure_v[x] = value

    out = pltpu.make_async_copy(pressure_v, pressure_h, local_sem.at[6])
    out.start()
    for item in sent:
        wait_sent(*item)

    @pl.loop(0, cx)
    def _(x):
        v1[x + 1, 0:cy] = pressure_v[x]

    to_rows(v1, 2)

    @pl.loop(0, cx)
    def _(x):
        c, image = operate(v1, x)
        final_v[x] = source_v[x] - image

    out2 = pltpu.make_async_copy(final_v, final_h, local_sem.at[7])
    out2.start()
    all_of(gm, (n - 1) * 8, 0).wait_send()
    all_of(gr, n - 1, 1).wait_send()
    out.wait()
    out2.wait()


def solution(mesh):
    ngx, ngy = mesh.shape["gx"], mesh.shape["gy"]

    def shards(perm, storage, source, weight, block_map, matrix):
        cx, cy, nz = perm.shape
        block = nz // matrix.shape[-1]
        n = ngx * ngy
        brick = pltpu.VMEM((cx, cy, nz), F32)
        padded = pltpu.VMEM((cx + 2, 16, nz), F32)
        face = pltpu.VMEM((2, cy, nz), F32)
        shape = jax.ShapeDtypeStruct(perm.shape, F32)
        return pl.pallas_call(
            functools.partial(kernel, ngx, ngy, block),
            out_shape=(shape, shape),
            in_specs=[pl.BlockSpec(memory_space=pltpu.HBM)] * 6,
            out_specs=[pl.BlockSpec(memory_space=pltpu.HBM)] * 2,
            scratch_shapes=[
                brick, brick, brick, brick, pltpu.VMEM((cx, cy, nz), jnp.int32),
                pltpu.VMEM(matrix.shape, F32),
                padded, padded, padded, pltpu.VMEM((cx + 1, 16, nz), F32),
                brick, brick, brick, brick, brick, brick,
                pltpu.VMEM((4, 2, cx, nz), F32), pltpu.VMEM((4, 2, cx, nz), F32),
                pltpu.VMEM((2, 2, 16, nz), F32),
                pltpu.VMEM((2, cx, nz), jnp.int32), pltpu.VMEM((2, cx, nz), jnp.int32),
                face, face, pltpu.VMEM((2, cy, nz), jnp.int32),
                pltpu.VMEM((8, 128), F32), pltpu.VMEM((n * 8, 128), F32),
                pltpu.VMEM((27, ngx, ngy, 128), F32),
                pltpu.VMEM((1, 128), F32), pltpu.VMEM((n, 1, 128), F32),
                pltpu.VMEM((ngx, ngy, 128), F32), pltpu.VMEM((16, nz), F32),
                pltpu.VMEM((nz, 128), jnp.bfloat16), pltpu.VMEM((128, nz), jnp.bfloat16),
                brick, brick,
                pltpu.SemaphoreType.DMA((8,)),
                pltpu.SemaphoreType.DMA((20,)), pltpu.SemaphoreType.DMA((20,)),
                pltpu.SemaphoreType.DMA((2,)), pltpu.SemaphoreType.DMA((2,)),
            ],
            compiler_params=pltpu.CompilerParams(
                collective_id=0, has_side_effects=True, vmem_limit_bytes=48 << 20
            ),
        )(perm, storage, source, weight, block_map, matrix)

    fine = P("gx", "gy", None)
    return jax.shard_map(
        shards,
        mesh=mesh,
        in_specs=(fine,) * 5 + (P(None, "gx", "gy", None),),
        out_specs=(fine, fine),
        check_vma=False,
    )
```

```python
import functools

import jax
import jax.numpy as jnp
from jax import lax
from jax.experimental import pallas as pl
from jax.experimental.pallas import tpu as pltpu
from jax.sharding import PartitionSpec as P

ITERS = 6
OMEGA = 0.8
MESH = pl.DeviceIdType.MESH
F32 = jnp.float32


def harmonic(a, b):
    return 2.0 * a * b / (a + b)


def pieces(value):
    high = value.astype(jnp.bfloat16).astype(F32)
    rest = value - high
    middle = rest.astype(jnp.bfloat16).astype(F32)
    return high, middle, rest - middle


def kernel(
    ngx, ngy, block,
    perm_h, storage_h, source_h, weight_h, map_h, matrix_h,
    pressure_h, final_h,
    perm_v, storage_v, source_v, weight_v, map_v, matrix_v,
    pad_p, v1, v2, tx, typ, tym, tzp, tzm, diag, inv,
    sy, ry, sx, sym, rym, px, wx, mx,
    tile, gm, coef, row, gr, field, spread, ind, indt,
    pressure_v, final_v,
    local_sem, send_sem, recv_sem, gsend_sem, grecv_sem,
):
    n = ngx * ngy
    cx, cy, nz = perm_v.shape
    blocks = matrix_v.shape[-1]
    gx, gy = lax.axis_index("gx"), lax.axis_index("gy")
    me = gx * ngy + gy
    has = (gy > 0, gy < ngy - 1, gx > 0, gx < ngx - 1)
    near = ((gx, gy - 1), (gx, gy + 1), (gx - 1, gy), (gx + 1, gy))

    loads = [
        pltpu.make_async_copy(src, dst, local_sem.at[i])
        for i, (src, dst) in enumerate((
            (perm_h, perm_v), (matrix_h, matrix_v), (source_h, source_v),
            (storage_h, storage_v), (weight_h, weight_v), (map_h, map_v),
        ))
    ]
    for load in loads:
        load.start()

    def other(k):
        t = lax.rem(me + k, n)
        return (t // ngy, lax.rem(t, ngy))

    barrier = pltpu.get_barrier_semaphore()

    @pl.loop(1, n)
    def _(k):
        pl.semaphore_signal(barrier, inc=1, device_id=other(k), device_id_type=MESH)

    for d in range(2):
        @pl.when(jnp.logical_not(has[d]))
        def _():
            for s in range(4):
                ry[s, d] = jnp.zeros(ry.shape[2:], F32)
            rym[d] = jnp.zeros(rym.shape[1:], jnp.int32)

        @pl.when(jnp.logical_not(has[2 + d]))
        def _():
            px[d] = jnp.zeros(px.shape[1:], F32)
            wx[d] = jnp.zeros(wx.shape[1:], F32)
            mx[d] = jnp.zeros(mx.shape[1:], jnp.int32)
            for v in (v1, v2):
                v[d * (cx + 1)] = jnp.zeros(v.shape[1:], F32)

    zid = lax.broadcasted_iota(jnp.int32, (nz, 128), 0) // block
    ind[...] = (zid == lax.broadcasted_iota(jnp.int32, (nz, 128), 1)).astype(F32).astype(jnp.bfloat16)
    zidt = lax.broadcasted_iota(jnp.int32, (128, nz), 1) // block
    indt[...] = (zidt == lax.broadcasted_iota(jnp.int32, (128, nz), 0)).astype(F32).astype(jnp.bfloat16)
    pad_p[...] = jnp.ones(pad_p.shape, F32)
    tile[...] = jnp.zeros(tile.shape, F32)
    sx[...] = jnp.zeros(sx.shape, F32)

    pl.semaphore_wait(barrier, n - 1)

    def halo(stage, d, src, dst):
        return pltpu.make_async_remote_copy(
            src_ref=src, dst_ref=dst,
            send_sem=send_sem.at[stage * 4 + d],
            recv_sem=recv_sem.at[stage * 4 + (d ^ 1)],
            device_id=near[d], device_id_type=MESH,
        )

    def send(stage, d, src, dst):
        @pl.when(has[d])
        def _():
            halo(stage, d, src, dst).start()

    def wait_sent(stage, d, src, dst):
        @pl.when(has[d])
        def _():
            halo(stage, d, src, dst).wait_send()

    def wait_halo(stage, d, dst):
        @pl.when(has[d])
        def _():
            pltpu.make_async_remote_copy(
                src_ref=dst, dst_ref=dst,
                send_sem=send_sem.at[stage * 4 + d],
                recv_sem=recv_sem.at[stage * 4 + d],
                device_id=near[d], device_id_type=MESH,
            ).wait_recv()

    sent = []

    def go(stage, d, src, dst):
        send(stage, d, src, dst)
        sent.append((stage, d, src, dst))

    for d in range(2):
        go(0, 2 + d, perm_h.at[(cx - 1) * d], px.at[d ^ 1])
    loads[0].wait()

    @pl.loop(0, cx)
    def _(x):
        p = perm_v[x]
        pad_p[x + 1, 0:cy] = p
        sy[0, 0, pl.ds(x, 1)] = p[0:1]
        sy[0, 1, pl.ds(x, 1)] = p[cy - 1 : cy]

    for d in range(2):
        go(0, d, sy.at[0, d], ry.at[0, d ^ 1])

    loads[1].wait()
    for p in range(7):
        tile[p : p + 1, 0:blocks] = matrix_v[p, 0]
        tile[p : p + 1, 64 : 64 + blocks] = matrix_v[p + 7, 0]

    def matrix_copy(k):
        return pltpu.make_async_remote_copy(
            src_ref=tile, dst_ref=gm.at[pl.ds(pl.multiple_of(me * 8, 8), 8)],
            send_sem=gsend_sem.at[0], recv_sem=grecv_sem.at[0],
            device_id=other(k), device_id_type=MESH,
        )

    loads[4].wait()
    loads[5].wait()

    @pl.loop(0, cx)
    def _(x):
        w = weight_v[x]
        sy[3, 0, pl.ds(x, 1)] = w[0:1]
        sy[3, 1, pl.ds(x, 1)] = w[cy - 1 : cy]
        m = map_v[x]
        sym[0, pl.ds(x, 1)] = m[0:1]
        sym[1, pl.ds(x, 1)] = m[cy - 1 : cy]

    loads[2].wait()
    loads[3].wait()

    for d in range(4):
        wait_halo(0, d, ry.at[0, d] if d < 2 else px.at[d - 2])

    def to_rows(buffer, stage):
        @pl.loop(0, cx)
        def _(x):
            buffer[x + 1, 15:16] = ry[stage, 0, pl.ds(x, 1)]
            buffer[x + 1, cy : cy + 1] = ry[stage, 1, pl.ds(x, 1)]

    pad_p[0, 0:cy] = px[0]
    pad_p[cx + 1, 0:cy] = px[1]
    to_rows(pad_p, 0)

    tx[0] = harmonic(pad_p[0], pad_p[1])
    lane = lax.broadcasted_iota(jnp.int32, (16, nz), 1)

    @pl.loop(0, cx)
    def _(x):
        p = pad_p[x + 1]
        up = harmonic(p, pad_p[x + 2])
        tx[x + 1] = up
        yp = harmonic(p, pltpu.roll(p, 15, 0))
        ym = pltpu.roll(yp, 1, 0)
        zp = jnp.where(lane == nz - 1, 0.0, harmonic(p, pltpu.roll(p, nz - 1, 1)))
        zm = pltpu.roll(zp, 1, 1)
        typ[x] = yp[0:cy]
        tym[x] = ym[0:cy]
        tzp[x] = zp[0:cy]
        tzm[x] = zm[0:cy]
        total = storage_v[x] + (up + tx[x] + yp + ym + zp + zm)[0:cy]
        inverse = 1.0 / total
        diag[x] = total
        inv[x] = inverse
        first = OMEGA * source_v[x] * inverse
        v1[x + 1, 0:cy] = first
        sy[1, 0, pl.ds(x, 1)] = first[0:1]
        sy[1, 1, pl.ds(x, 1)] = first[cy - 1 : cy]

    def field_halo(stage, v):
        for d in range(2):
            go(stage, d, sy.at[stage, d], ry.at[stage, d ^ 1])
        for d in range(2):
            sx[stage - 1, d, 0:cy] = v[1 + (cx - 1) * d, 0:cy]
            go(stage, 2 + d, sx.at[stage - 1, d], v.at[(cx + 1) * (1 - d)])

    def field_wait(stage, v):
        for d in range(4):
            wait_halo(stage, d, ry.at[stage, d] if d < 2 else v.at[(cx + 1) * (d - 2)])

    def operate(v, x):
        c = v[x + 1]
        total = tx[x + 1, 0:cy] * v[x + 2, 0:cy] + tx[x, 0:cy] * v[x, 0:cy]
        total += typ[x] * pltpu.roll(c, 15, 0)[0:cy] + tym[x] * pltpu.roll(c, 1, 0)[0:cy]
        total += tzp[x] * pltpu.roll(c, nz - 1, 1)[0:cy] + tzm[x] * pltpu.roll(c, 1, 1)[0:cy]
        return c[0:cy], diag[x] * c[0:cy] - total

    field_halo(1, v1)

    @pl.loop(1, n)
    def _(k):
        matrix_copy(k).start()

    gm[pl.ds(pl.multiple_of(me * 8, 8), 8)] = tile[...]

    field_wait(1, v1)
    to_rows(v1, 1)

    @pl.loop(0, cx)
    def _(x):
        c, image = operate(v1, x)
        second = c + OMEGA * (source_v[x] - image) * inv[x]
        v2[x + 1, 0:cy] = second
        sy[2, 0, pl.ds(x, 1)] = second[0:1]
        sy[2, 1, pl.ds(x, 1)] = second[cy - 1 : cy]

    field_halo(2, v2)

    for d in range(2):
        go(3, d, sy.at[3, d], ry.at[3, d ^ 1])
        go(4, d, sym.at[d], rym.at[d ^ 1])
        go(3, 2 + d, weight_h.at[(cx - 1) * d], wx.at[d ^ 1])
        go(4, 2 + d, map_h.at[(cx - 1) * d], mx.at[d ^ 1])

    field_wait(2, v2)
    to_rows(v2, 2)

    zblock = lax.broadcasted_iota(jnp.int32, (cy, nz), 1) // block

    def gather(x, carry):
        same, before = carry
        c, image = operate(v2, x)
        value = weight_v[x] * (source_v[x] - image)
        here = map_v[x] == zblock
        return same + jnp.where(here, value, 0.0), before + jnp.where(here, 0.0, value)

    zero = jnp.zeros((cy, nz), F32)
    same, before = lax.fori_loop(0, cx, gather, (zero, zero))
    same = jnp.broadcast_to(jnp.sum(same, axis=0, keepdims=True), (16, nz))
    before = jnp.broadcast_to(jnp.sum(before, axis=0, keepdims=True), (16, nz))
    high, middle, low = pieces(same + pltpu.roll(before, nz - 1, 1))
    rows = lax.broadcasted_iota(jnp.int32, (16, nz), 0)
    stacked = jnp.where(rows == 0, high, jnp.where(rows == 1, middle, jnp.where(rows == 2, low, 0.0)))
    sums = jnp.dot(stacked.astype(jnp.bfloat16), ind[...], preferred_element_type=F32)
    mine = jnp.sum(sums, axis=0, keepdims=True)
    row[...] = mine

    def row_copy(k):
        return pltpu.make_async_remote_copy(
            src_ref=row, dst_ref=gr.at[me],
            send_sem=gsend_sem.at[1], recv_sem=grecv_sem.at[1],
            device_id=other(k), device_id_type=MESH,
        )

    @pl.loop(1, n)
    def _(k):
        row_copy(k).start()

    gr[me] = mine

    def all_of(buffer, size, which):
        part = buffer.at[pl.ds(0, size)]
        return pltpu.make_async_remote_copy(
            src_ref=part, dst_ref=part,
            send_sem=gsend_sem.at[which], recv_sem=grecv_sem.at[which],
            device_id=other(1), device_id_type=MESH,
        )

    all_of(gm, (n - 1) * 8, 0).wait_recv()
    lower = lax.broadcasted_iota(jnp.int32, (ngy, 128), 1) < 64
    for p in range(7):
        for g in range(ngx):
            both = gm[pl.ds(g * ngy * 8 + p, ngy, stride=8), :]
            coef[p, g] = jnp.where(lower, both, 0.0)
            coef[p + 7, g] = jnp.where(lower, pltpu.roll(both, 64, 1), 0.0)

    def moved(plane, dy, dz):
        if dz:
            plane = pltpu.roll(plane, dz % 128, 1)
        if dy:
            plane = pltpu.roll(plane, dy % ngy, 0)
        return plane

    for o in range(13):
        dx, dy, dz = o // 9 - 1, o // 3 % 3 - 1, o % 3 - 1
        for g in range(ngx):
            coef[26 - o, g] = moved(coef[o, (g - dx) % ngx], dy, dz)

    all_of(gr, n - 1, 1).wait_recv()
    for g in range(ngx):
        for h in range(ngy):
            field[g, h : h + 1] = gr[g * ngy + h]

    def apply(u):
        result = [None] * ngx
        for dy in (-1, 0, 1):
            for dz in (-1, 0, 1):
                shifted = [moved(plane, -dy, -dz) for plane in u]
                for dx in (-1, 0, 1):
                    o = 9 * (dx + 1) + 3 * (dy + 1) + dz + 1
                    for g in range(ngx):
                        if 0 <= g + dx < ngx:
                            term = coef[o, g] * shifted[g + dx]
                            result[g] = term if result[g] is None else result[g] + term
        return result

    def inner(a, b):
        total = a[0] * b[0]
        for g in range(1, ngx):
            total = total + a[g] * b[g]
        return jnp.sum(jnp.sum(total, axis=0, keepdims=True), axis=1, keepdims=True)

    residual = [field[g] for g in range(ngx)]
    direction = residual
    answer = [jnp.zeros((ngy, 128), F32)] * ngx
    norm = inner(residual, residual)
    for iteration in range(ITERS):
        applied = apply(direction)
        step = norm / inner(direction, applied)
        answer = [a + step * b for a, b in zip(answer, direction)]
        if iteration + 1 < ITERS:
            residual = [a - step * b for a, b in zip(residual, applied)]
            following = inner(residual, residual)
            ratio = following / norm
            direction = [a + ratio * b for a, b in zip(residual, direction)]
            norm = following
    for g in range(ngx):
        field[g] = answer[g]

    west, east = jnp.maximum(gx - 1, 0), jnp.minimum(gx + 1, ngx - 1)
    south, north = jnp.maximum(gy - 1, 0), jnp.minimum(gy + 1, ngy - 1)
    picks = ((gx, gy), (gx, south), (gx, north), (west, gy), (east, gy))
    rows = lax.broadcasted_iota(jnp.int32, (16, 128), 0)
    stacked = jnp.zeros((16, 128), F32)
    for i, (a, b) in enumerate(picks):
        value = jnp.broadcast_to(field[a, pl.ds(b, 1)], (16, 128))
        for j, piece in enumerate(pieces(value)):
            stacked = jnp.where(rows == 3 * i + j, piece, stacked)
    spread[...] = jnp.dot(stacked.astype(jnp.bfloat16), indt[...], preferred_element_type=F32)

    def by_block(i):
        value = spread[3 * i : 3 * i + 1] + spread[3 * i + 1 : 3 * i + 2] + spread[3 * i + 2 : 3 * i + 3]
        value = jnp.broadcast_to(value, (16, nz))
        return value[0:cy], pltpu.roll(value, 1, 1)[0:cy]

    for d in range(4):
        wait_halo(3, d, ry.at[3, d] if d < 2 else wx.at[d - 2])
        wait_halo(4, d, rym.at[d] if d < 2 else mx.at[d - 2])

    for d in range(2):
        now, prior = by_block(1 + d)
        ry[2, d] = ry[2, d] + ry[3, d] * jnp.where(rym[d] == zblock, now, prior)
        now, prior = by_block(3 + d)
        at = d * (cx + 1)
        v1[at, 0:cy] = v2[at, 0:cy] + wx[d] * jnp.where(mx[d] == zblock, now, prior)

    now, prior = by_block(0)

    @pl.loop(0, cx)
    def _(x):
        value = v2[x + 1, 0:cy] + weight_v[x] * jnp.where(map_v[x] == zblock, now, prior)
        pressure_v[x] = value

    out = pltpu.make_async_copy(pressure_v, pressure_h, local_sem.at[6])
    out.start()
    for item in sent:
        wait_sent(*item)

    @pl.loop(0, cx)
    def _(x):
        v1[x + 1, 0:cy] = pressure_v[x]

    to_rows(v1, 2)

    @pl.loop(0, cx)
    def _(x):
        c, image = operate(v1, x)
        final_v[x] = source_v[x] - image

    out2 = pltpu.make_async_copy(final_v, final_h, local_sem.at[7])
    out2.start()
    all_of(gm, (n - 1) * 8, 0).wait_send()
    all_of(gr, n - 1, 1).wait_send()
    out.wait()
    out2.wait()


def solution(mesh):
    ngx, ngy = mesh.shape["gx"], mesh.shape["gy"]

    def shards(perm, storage, source, weight, block_map, matrix):
        cx, cy, nz = perm.shape
        block = nz // matrix.shape[-1]
        n = ngx * ngy
        brick = pltpu.VMEM((cx, cy, nz), F32)
        padded = pltpu.VMEM((cx + 2, 16, nz), F32)
        face = pltpu.VMEM((2, cy, nz), F32)
        shape = jax.ShapeDtypeStruct(perm.shape, F32)
        return pl.pallas_call(
            functools.partial(kernel, ngx, ngy, block),
            out_shape=(shape, shape),
            in_specs=[pl.BlockSpec(memory_space=pltpu.HBM)] * 6,
            out_specs=[pl.BlockSpec(memory_space=pltpu.HBM)] * 2,
            scratch_shapes=[
                brick, brick, brick, brick, pltpu.VMEM((cx, cy, nz), jnp.int32),
                pltpu.VMEM(matrix.shape, F32),
                padded, padded, padded, pltpu.VMEM((cx + 1, 16, nz), F32),
                brick, brick, brick, brick, brick, brick,
                pltpu.VMEM((4, 2, cx, nz), F32), pltpu.VMEM((4, 2, cx, nz), F32),
                pltpu.VMEM((2, 2, 16, nz), F32),
                pltpu.VMEM((2, cx, nz), jnp.int32), pltpu.VMEM((2, cx, nz), jnp.int32),
                face, face, pltpu.VMEM((2, cy, nz), jnp.int32),
                pltpu.VMEM((8, 128), F32), pltpu.VMEM((n * 8, 128), F32),
                pltpu.VMEM((27, ngx, ngy, 128), F32),
                pltpu.VMEM((1, 128), F32), pltpu.VMEM((n, 1, 128), F32),
                pltpu.VMEM((ngx, ngy, 128), F32), pltpu.VMEM((16, nz), F32),
                pltpu.VMEM((nz, 128), jnp.bfloat16), pltpu.VMEM((128, nz), jnp.bfloat16),
                brick, brick,
                pltpu.SemaphoreType.DMA((8,)),
                pltpu.SemaphoreType.DMA((20,)), pltpu.SemaphoreType.DMA((20,)),
                pltpu.SemaphoreType.DMA((2,)), pltpu.SemaphoreType.DMA((2,)),
            ],
            compiler_params=pltpu.CompilerParams(
                collective_id=0, has_side_effects=True, vmem_limit_bytes=63 << 20
            ),
        )(perm, storage, source, weight, block_map, matrix)

    fine = P("gx", "gy", None)
    return jax.shard_map(
        shards,
        mesh=mesh,
        in_specs=(fine,) * 5 + (P(None, "gx", "gy", None),),
        out_specs=(fine, fine),
        check_vma=False,
    )
```

```python
import functools

import jax
import jax.numpy as jnp
from jax import lax
from jax.experimental import pallas as pl
from jax.experimental.pallas import tpu as pltpu
from jax.sharding import PartitionSpec as P

ITERS = 6
OMEGA = 0.8
MESH = pl.DeviceIdType.MESH
F32 = jnp.float32


def harmonic(a, b):
    return 2.0 * a * b / (a + b)


def pieces(value):
    high = value.astype(jnp.bfloat16).astype(F32)
    rest = value - high
    middle = rest.astype(jnp.bfloat16).astype(F32)
    return high, middle, rest - middle


def kernel(
    ngx, ngy, block,
    perm_h, storage_h, source_h, weight_h, map_h, matrix_h,
    pressure_h, final_h,
    perm_v, storage_v, source_v, weight_v, map_v, matrix_v,
    pad_p, v1, v2, tx, typ, tym, tzp, tzm, diag, inv,
    sy, ry, sx, sym, rym, px, wx, mx,
    tile, gm, coef, row, gr, field, spread, ind, indt,
    pressure_v, final_v,
    local_sem, send_sem, recv_sem, gsend_sem, grecv_sem,
):
    n = ngx * ngy
    cx, cy, nz = perm_v.shape
    blocks = matrix_v.shape[-1]
    gx, gy = lax.axis_index("gx"), lax.axis_index("gy")
    me = gx * ngy + gy
    has = (gy > 0, gy < ngy - 1, gx > 0, gx < ngx - 1)
    near = ((gx, gy - 1), (gx, gy + 1), (gx - 1, gy), (gx + 1, gy))

    loads = [
        pltpu.make_async_copy(src, dst, local_sem.at[i])
        for i, (src, dst) in enumerate((
            (perm_h, perm_v), (matrix_h, matrix_v), (source_h, source_v),
            (storage_h, storage_v), (weight_h, weight_v), (map_h, map_v),
        ))
    ]
    for load in loads:
        load.start()

    def around(at, step, size):
        moved_on = at + step
        return jnp.where(moved_on >= size, moved_on - size, moved_on)

    def for_others(act):
        steps = [(a, b) for a in range(ngx) for b in range(ngy) if a or b]
        if n <= 64:
            steps.sort(key=lambda step: -min(step[1], ngy - step[1]))
            for a, b in steps:
                act((around(gx, a, ngx), around(gy, b, ngy)))
        else:
            @pl.loop(1, n)
            def _(k):
                t = lax.rem(me + k, n)
                act((t // ngy, lax.rem(t, ngy)))

    barrier = pltpu.get_barrier_semaphore()

    for_others(lambda t: pl.semaphore_signal(barrier, inc=1, device_id=t, device_id_type=MESH))

    for d in range(2):
        @pl.when(jnp.logical_not(has[d]))
        def _():
            for s in range(4):
                ry[s, d] = jnp.zeros(ry.shape[2:], F32)
            rym[d] = jnp.zeros(rym.shape[1:], jnp.int32)

        @pl.when(jnp.logical_not(has[2 + d]))
        def _():
            px[d] = jnp.zeros(px.shape[1:], F32)
            wx[d] = jnp.zeros(wx.shape[1:], F32)
            mx[d] = jnp.zeros(mx.shape[1:], jnp.int32)
            for v in (v1, v2):
                v[d * (cx + 1)] = jnp.zeros(v.shape[1:], F32)

    def inside(shape, z_dim):
        z = lax.broadcasted_iota(jnp.int32, shape, z_dim)
        offset = z - block * lax.broadcasted_iota(jnp.int32, shape, 1 - z_dim)
        return ((offset >= 0) & (offset < block)).astype(F32).astype(jnp.bfloat16)

    ind[...] = inside((nz, 128), 0)
    indt[...] = inside((128, nz), 1)
    pad_p[...] = jnp.ones(pad_p.shape, F32)
    tile[...] = jnp.zeros(tile.shape, F32)
    sx[...] = jnp.zeros(sx.shape, F32)

    pl.semaphore_wait(barrier, n - 1)

    def halo(stage, d, src, dst):
        return pltpu.make_async_remote_copy(
            src_ref=src, dst_ref=dst,
            send_sem=send_sem.at[stage * 4 + d],
            recv_sem=recv_sem.at[stage * 4 + (d ^ 1)],
            device_id=near[d], device_id_type=MESH,
        )

    def send(stage, d, src, dst):
        @pl.when(has[d])
        def _():
            halo(stage, d, src, dst).start()

    def wait_sent(stage, d, src, dst):
        @pl.when(has[d])
        def _():
            halo(stage, d, src, dst).wait_send()

    def wait_halo(stage, d, dst):
        @pl.when(has[d])
        def _():
            pltpu.make_async_remote_copy(
                src_ref=dst, dst_ref=dst,
                send_sem=send_sem.at[stage * 4 + d],
                recv_sem=recv_sem.at[stage * 4 + d],
                device_id=near[d], device_id_type=MESH,
            ).wait_recv()

    sent = []

    def go(stage, d, src, dst):
        send(stage, d, src, dst)
        sent.append((stage, d, src, dst))

    for d in range(2):
        go(0, 2 + d, perm_h.at[(cx - 1) * d], px.at[d ^ 1])
    loads[0].wait()

    @pl.loop(0, cx)
    def _(x):
        p = perm_v[x]
        pad_p[x + 1, 0:cy] = p
        sy[0, 0, pl.ds(x, 1)] = p[0:1]
        sy[0, 1, pl.ds(x, 1)] = p[cy - 1 : cy]

    for d in range(2):
        go(0, d, sy.at[0, d], ry.at[0, d ^ 1])

    loads[1].wait()
    for p in range(7):
        tile[p : p + 1, 0:blocks] = matrix_v[p, 0]
        tile[p : p + 1, 64 : 64 + blocks] = matrix_v[p + 7, 0]

    def matrix_copy(target):
        return pltpu.make_async_remote_copy(
            src_ref=tile, dst_ref=gm.at[pl.ds(pl.multiple_of(me * 8, 8), 8)],
            send_sem=gsend_sem.at[0], recv_sem=grecv_sem.at[0],
            device_id=target, device_id_type=MESH,
        )

    loads[4].wait()
    loads[5].wait()

    @pl.loop(0, cx)
    def _(x):
        w = weight_v[x]
        sy[3, 0, pl.ds(x, 1)] = w[0:1]
        sy[3, 1, pl.ds(x, 1)] = w[cy - 1 : cy]
        m = map_v[x]
        sym[0, pl.ds(x, 1)] = m[0:1]
        sym[1, pl.ds(x, 1)] = m[cy - 1 : cy]

    loads[2].wait()
    loads[3].wait()

    for d in range(4):
        wait_halo(0, d, ry.at[0, d] if d < 2 else px.at[d - 2])

    for d in range(2):
        go(3, d, sy.at[3, d], ry.at[3, d ^ 1])
        go(4, d, sym.at[d], rym.at[d ^ 1])
        go(3, 2 + d, weight_h.at[(cx - 1) * d], wx.at[d ^ 1])
        go(4, 2 + d, map_h.at[(cx - 1) * d], mx.at[d ^ 1])

    def to_rows(buffer, stage):
        @pl.loop(0, cx)
        def _(x):
            buffer[x + 1, 15:16] = ry[stage, 0, pl.ds(x, 1)]
            buffer[x + 1, cy : cy + 1] = ry[stage, 1, pl.ds(x, 1)]

    pad_p[0, 0:cy] = px[0]
    pad_p[cx + 1, 0:cy] = px[1]
    to_rows(pad_p, 0)

    tx[0] = harmonic(pad_p[0], pad_p[1])
    lane = lax.broadcasted_iota(jnp.int32, (16, nz), 1)

    @pl.loop(0, cx)
    def _(x):
        p = pad_p[x + 1]
        up = harmonic(p, pad_p[x + 2])
        tx[x + 1] = up
        yp = harmonic(p, pltpu.roll(p, 15, 0))
        ym = pltpu.roll(yp, 1, 0)
        zp = jnp.where(lane == nz - 1, 0.0, harmonic(p, pltpu.roll(p, nz - 1, 1)))
        zm = pltpu.roll(zp, 1, 1)
        typ[x] = yp[0:cy]
        tym[x] = ym[0:cy]
        tzp[x] = zp[0:cy]
        tzm[x] = zm[0:cy]
        total = storage_v[x] + (up + tx[x] + yp + ym + zp + zm)[0:cy]
        inverse = 1.0 / total
        diag[x] = total
        inv[x] = inverse
        first = OMEGA * source_v[x] * inverse
        v1[x + 1, 0:cy] = first
        sy[1, 0, pl.ds(x, 1)] = first[0:1]
        sy[1, 1, pl.ds(x, 1)] = first[cy - 1 : cy]

    def field_halo(stage, v):
        for d in range(2):
            go(stage, d, sy.at[stage, d], ry.at[stage, d ^ 1])
        for d in range(2):
            sx[stage - 1, d, 0:cy] = v[1 + (cx - 1) * d, 0:cy]
            go(stage, 2 + d, sx.at[stage - 1, d], v.at[(cx + 1) * (1 - d)])

    def field_wait(stage, v):
        for d in range(4):
            wait_halo(stage, d, ry.at[stage, d] if d < 2 else v.at[(cx + 1) * (d - 2)])

    def operate(v, x):
        c = v[x + 1]
        total = tx[x + 1, 0:cy] * v[x + 2, 0:cy] + tx[x, 0:cy] * v[x, 0:cy]
        total += typ[x] * pltpu.roll(c, 15, 0)[0:cy] + tym[x] * pltpu.roll(c, 1, 0)[0:cy]
        total += tzp[x] * pltpu.roll(c, nz - 1, 1)[0:cy] + tzm[x] * pltpu.roll(c, 1, 1)[0:cy]
        return c[0:cy], diag[x] * c[0:cy] - total

    field_halo(1, v1)

    for_others(lambda t: matrix_copy(t).start())

    gm[pl.ds(pl.multiple_of(me * 8, 8), 8)] = tile[...]

    field_wait(1, v1)
    to_rows(v1, 1)

    @pl.loop(0, cx)
    def _(x):
        c, image = operate(v1, x)
        second = c + OMEGA * (source_v[x] - image) * inv[x]
        v2[x + 1, 0:cy] = second
        sy[2, 0, pl.ds(x, 1)] = second[0:1]
        sy[2, 1, pl.ds(x, 1)] = second[cy - 1 : cy]

    field_halo(2, v2)

    field_wait(2, v2)
    to_rows(v2, 2)

    zline = lax.broadcasted_iota(jnp.int32, (cy, nz), 1)

    def is_here(cell_map):
        return zline - block * cell_map < block


    def gather(x, carry):
        same, before = carry
        c, image = operate(v2, x)
        value = weight_v[x] * (source_v[x] - image)
        here = is_here(map_v[x])
        return same + jnp.where(here, value, 0.0), before + jnp.where(here, 0.0, value)

    zero = jnp.zeros((cy, nz), F32)
    same, before = lax.fori_loop(0, cx, gather, (zero, zero))
    same = jnp.broadcast_to(jnp.sum(same, axis=0, keepdims=True), (16, nz))
    before = jnp.broadcast_to(jnp.sum(before, axis=0, keepdims=True), (16, nz))
    high, middle, low = pieces(same + pltpu.roll(before, nz - 1, 1))
    rows = lax.broadcasted_iota(jnp.int32, (16, nz), 0)
    stacked = jnp.where(rows == 0, high, jnp.where(rows == 1, middle, jnp.where(rows == 2, low, 0.0)))
    sums = jnp.dot(stacked.astype(jnp.bfloat16), ind[...], preferred_element_type=F32)
    mine = jnp.sum(sums, axis=0, keepdims=True)
    row[...] = mine

    def row_copy(target):
        return pltpu.make_async_remote_copy(
            src_ref=row, dst_ref=gr.at[me],
            send_sem=gsend_sem.at[1], recv_sem=grecv_sem.at[1],
            device_id=target, device_id_type=MESH,
        )

    for_others(lambda t: row_copy(t).start())

    gr[me] = mine

    def all_of(buffer, size, which):
        part = buffer.at[pl.ds(0, size)]
        return pltpu.make_async_remote_copy(
            src_ref=part, dst_ref=part,
            send_sem=gsend_sem.at[which], recv_sem=grecv_sem.at[which],
            device_id=(around(gx, 1, ngx), gy), device_id_type=MESH,
        )

    all_of(gm, (n - 1) * 8, 0).wait_recv()
    lower = lax.broadcasted_iota(jnp.int32, (ngy, 128), 1) < 64
    for p in range(7):
        for g in range(ngx):
            both = gm[pl.ds(g * ngy * 8 + p, ngy, stride=8), :]
            coef[p, g] = jnp.where(lower, both, 0.0)
            coef[p + 7, g] = jnp.where(lower, pltpu.roll(both, 64, 1), 0.0)

    def moved(plane, dy, dz):
        if dz:
            plane = pltpu.roll(plane, dz % 128, 1)
        if dy:
            plane = pltpu.roll(plane, dy % ngy, 0)
        return plane

    for o in range(13):
        dx, dy, dz = o // 9 - 1, o // 3 % 3 - 1, o % 3 - 1
        for g in range(ngx):
            coef[26 - o, g] = moved(coef[o, (g - dx) % ngx], dy, dz)

    all_of(gr, n - 1, 1).wait_recv()
    for g in range(ngx):
        for h in range(ngy):
            field[g, h : h + 1] = gr[g * ngy + h]

    def apply(u):
        result = [None] * ngx
        for dy in (-1, 0, 1):
            for dz in (-1, 0, 1):
                shifted = [moved(plane, -dy, -dz) for plane in u]
                for dx in (-1, 0, 1):
                    o = 9 * (dx + 1) + 3 * (dy + 1) + dz + 1
                    for g in range(ngx):
                        if 0 <= g + dx < ngx:
                            term = coef[o, g] * shifted[g + dx]
                            result[g] = term if result[g] is None else result[g] + term
        return result

    def inner(a, b):
        total = a[0] * b[0]
        for g in range(1, ngx):
            total = total + a[g] * b[g]
        return jnp.sum(jnp.sum(total, axis=0, keepdims=True), axis=1, keepdims=True)

    residual = [field[g] for g in range(ngx)]
    direction = residual
    answer = [jnp.zeros((ngy, 128), F32)] * ngx
    norm = inner(residual, residual)
    for iteration in range(ITERS):
        applied = apply(direction)
        step = norm / inner(direction, applied)
        answer = [a + step * b for a, b in zip(answer, direction)]
        if iteration + 1 < ITERS:
            residual = [a - step * b for a, b in zip(residual, applied)]
            following = inner(residual, residual)
            ratio = following / norm
            direction = [a + ratio * b for a, b in zip(residual, direction)]
            norm = following
    for g in range(ngx):
        field[g] = answer[g]

    west, east = jnp.maximum(gx - 1, 0), jnp.minimum(gx + 1, ngx - 1)
    south, north = jnp.maximum(gy - 1, 0), jnp.minimum(gy + 1, ngy - 1)
    picks = ((gx, gy), (gx, south), (gx, north), (west, gy), (east, gy))
    rows = lax.broadcasted_iota(jnp.int32, (16, 128), 0)
    stacked = jnp.zeros((16, 128), F32)
    for i, (a, b) in enumerate(picks):
        value = jnp.broadcast_to(field[a, pl.ds(b, 1)], (16, 128))
        for j, piece in enumerate(pieces(value)):
            stacked = jnp.where(rows == 3 * i + j, piece, stacked)
    spread[...] = jnp.dot(stacked.astype(jnp.bfloat16), indt[...], preferred_element_type=F32)

    def by_block(i):
        value = spread[3 * i : 3 * i + 1] + spread[3 * i + 1 : 3 * i + 2] + spread[3 * i + 2 : 3 * i + 3]
        value = jnp.broadcast_to(value, (16, nz))
        return value[0:cy], pltpu.roll(value, 1, 1)[0:cy]

    for d in range(4):
        wait_halo(3, d, ry.at[3, d] if d < 2 else wx.at[d - 2])
        wait_halo(4, d, rym.at[d] if d < 2 else mx.at[d - 2])

    for d in range(2):
        now, prior = by_block(1 + d)
        ry[2, d] = ry[2, d] + ry[3, d] * jnp.where(is_here(rym[d]), now, prior)
        now, prior = by_block(3 + d)
        at = d * (cx + 1)
        v1[at, 0:cy] = v2[at, 0:cy] + wx[d] * jnp.where(is_here(mx[d]), now, prior)

    now, prior = by_block(0)

    @pl.loop(0, cx)
    def _(x):
        value = v2[x + 1, 0:cy] + weight_v[x] * jnp.where(is_here(map_v[x]), now, prior)
        pressure_v[x] = value

    out = pltpu.make_async_copy(pressure_v, pressure_h, local_sem.at[6])
    out.start()
    for item in sent:
        wait_sent(*item)

    @pl.loop(0, cx)
    def _(x):
        v1[x + 1, 0:cy] = pressure_v[x]

    to_rows(v1, 2)

    @pl.loop(0, cx)
    def _(x):
        c, image = operate(v1, x)
        final_v[x] = source_v[x] - image

    out2 = pltpu.make_async_copy(final_v, final_h, local_sem.at[7])
    out2.start()
    all_of(gm, (n - 1) * 8, 0).wait_send()
    all_of(gr, n - 1, 1).wait_send()
    out.wait()
    out2.wait()


def solution(mesh):
    ngx, ngy = mesh.shape["gx"], mesh.shape["gy"]

    def shards(perm, storage, source, weight, block_map, matrix):
        cx, cy, nz = perm.shape
        block = nz // matrix.shape[-1]
        n = ngx * ngy
        brick = pltpu.VMEM((cx, cy, nz), F32)
        padded = pltpu.VMEM((cx + 2, 16, nz), F32)
        face = pltpu.VMEM((2, cy, nz), F32)
        shape = jax.ShapeDtypeStruct(perm.shape, F32)
        return pl.pallas_call(
            functools.partial(kernel, ngx, ngy, block),
            out_shape=(shape, shape),
            in_specs=[pl.BlockSpec(memory_space=pltpu.HBM)] * 6,
            out_specs=[pl.BlockSpec(memory_space=pltpu.HBM)] * 2,
            scratch_shapes=[
                brick, brick, brick, brick, pltpu.VMEM((cx, cy, nz), jnp.int32),
                pltpu.VMEM(matrix.shape, F32),
                padded, padded, padded, pltpu.VMEM((cx + 1, 16, nz), F32),
                brick, brick, brick, brick, brick, brick,
                pltpu.VMEM((4, 2, cx, nz), F32), pltpu.VMEM((4, 2, cx, nz), F32),
                pltpu.VMEM((2, 2, 16, nz), F32),
                pltpu.VMEM((2, cx, nz), jnp.int32), pltpu.VMEM((2, cx, nz), jnp.int32),
                face, face, pltpu.VMEM((2, cy, nz), jnp.int32),
                pltpu.VMEM((8, 128), F32), pltpu.VMEM((n * 8, 128), F32),
                pltpu.VMEM((27, ngx, ngy, 128), F32),
                pltpu.VMEM((1, 128), F32), pltpu.VMEM((n, 1, 128), F32),
                pltpu.VMEM((ngx, ngy, 128), F32), pltpu.VMEM((16, nz), F32),
                pltpu.VMEM((nz, 128), jnp.bfloat16), pltpu.VMEM((128, nz), jnp.bfloat16),
                brick, brick,
                pltpu.SemaphoreType.DMA((8,)),
                pltpu.SemaphoreType.DMA((20,)), pltpu.SemaphoreType.DMA((20,)),
                pltpu.SemaphoreType.DMA((2,)), pltpu.SemaphoreType.DMA((2,)),
            ],
            compiler_params=pltpu.CompilerParams(
                collective_id=0, has_side_effects=True, vmem_limit_bytes=63 << 20
            ),
        )(perm, storage, source, weight, block_map, matrix)

    fine = P("gx", "gy", None)
    return jax.shard_map(
        shards,
        mesh=mesh,
        in_specs=(fine,) * 5 + (P(None, "gx", "gy", None),),
        out_specs=(fine, fine),
        check_vma=False,
    )
```

```python
import functools

import jax
import jax.numpy as jnp
from jax import lax
from jax.experimental import pallas as pl
from jax.experimental.pallas import tpu as pltpu
from jax.sharding import PartitionSpec as P

ITERS = 6
OMEGA = 0.8
MESH = pl.DeviceIdType.MESH
F32 = jnp.float32


def harmonic(a, b):
    return 2.0 * a * b / (a + b)


def pieces(value):
    high = value.astype(jnp.bfloat16).astype(F32)
    rest = value - high
    middle = rest.astype(jnp.bfloat16).astype(F32)
    return high, middle, rest - middle


def kernel(
    ngx, ngy, block,
    perm_h, storage_h, source_h, weight_h, map_h, matrix_h,
    pressure_h, final_h,
    perm_v, storage_v, source_v, weight_v, map_v, matrix_v,
    pad_p, v1, v2, tx, typ, tym, tzp, tzm, diag, inv,
    sy, ry, sx, sym, rym, px, wx, mx,
    tile, gm, coef, row, gr, field, spread, ind, indt,
    pressure_v, final_v,
    local_sem, send_sem, recv_sem, gsend_sem, grecv_sem,
):
    cx, cy, nz = perm_v.shape
    blocks = matrix_v.shape[-1]
    gx, gy = lax.axis_index("gx"), lax.axis_index("gy")
    has = (gy > 0, gy < ngy - 1, gx > 0, gx < ngx - 1)
    near = ((gx, gy - 1), (gx, gy + 1), (gx - 1, gy), (gx + 1, gy))

    loads = [
        pltpu.make_async_copy(src, dst, local_sem.at[i])
        for i, (src, dst) in enumerate((
            (perm_h, perm_v), (matrix_h, matrix_v), (source_h, source_v),
            (storage_h, storage_v), (weight_h, weight_v), (map_h, map_v),
        ))
    ]
    for load in loads:
        load.start()

    def around(at, step, size):
        moved_on = at + step
        return jnp.where(moved_on >= size, moved_on - size, moved_on)

    along_x = [(around(gx, a, ngx), gy) for a in range(1, ngx)]
    along_y = [(gx, around(gy, b, ngy)) for b in range(1, ngy)]

    barrier = pltpu.get_barrier_semaphore()

    for t in along_x + along_y:
        pl.semaphore_signal(barrier, inc=1, device_id=t, device_id_type=MESH)

    for d in range(2):
        @pl.when(jnp.logical_not(has[d]))
        def _():
            for s in range(4):
                ry[s, d] = jnp.zeros(ry.shape[2:], F32)
            rym[d] = jnp.zeros(rym.shape[1:], jnp.int32)

        @pl.when(jnp.logical_not(has[2 + d]))
        def _():
            px[d] = jnp.zeros(px.shape[1:], F32)
            wx[d] = jnp.zeros(wx.shape[1:], F32)
            mx[d] = jnp.zeros(mx.shape[1:], jnp.int32)
            for v in (v1, v2):
                v[d * (cx + 1)] = jnp.zeros(v.shape[1:], F32)

    def inside(shape, z_dim):
        z = lax.broadcasted_iota(jnp.int32, shape, z_dim)
        offset = z - block * lax.broadcasted_iota(jnp.int32, shape, 1 - z_dim)
        return ((offset >= 0) & (offset < block)).astype(F32).astype(jnp.bfloat16)

    ind[...] = inside((nz, 128), 0)
    indt[...] = inside((128, nz), 1)
    pad_p[...] = jnp.ones(pad_p.shape, F32)
    tile[...] = jnp.zeros(tile.shape, F32)
    sx[...] = jnp.zeros(sx.shape, F32)

    pl.semaphore_wait(barrier, ngx + ngy - 2)

    def halo(stage, d, src, dst):
        return pltpu.make_async_remote_copy(
            src_ref=src, dst_ref=dst,
            send_sem=send_sem.at[stage * 4 + d],
            recv_sem=recv_sem.at[stage * 4 + (d ^ 1)],
            device_id=near[d], device_id_type=MESH,
        )

    def send(stage, d, src, dst):
        @pl.when(has[d])
        def _():
            halo(stage, d, src, dst).start()

    def wait_sent(stage, d, src, dst):
        @pl.when(has[d])
        def _():
            halo(stage, d, src, dst).wait_send()

    def wait_halo(stage, d, dst):
        @pl.when(has[d])
        def _():
            pltpu.make_async_remote_copy(
                src_ref=dst, dst_ref=dst,
                send_sem=send_sem.at[stage * 4 + d],
                recv_sem=recv_sem.at[stage * 4 + d],
                device_id=near[d], device_id_type=MESH,
            ).wait_recv()

    sent = []

    def go(stage, d, src, dst):
        send(stage, d, src, dst)
        sent.append((stage, d, src, dst))

    for d in range(2):
        go(0, 2 + d, perm_h.at[(cx - 1) * d], px.at[d ^ 1])
    loads[0].wait()

    @pl.loop(0, cx)
    def _(x):
        p = perm_v[x]
        pad_p[x + 1, 0:cy] = p
        sy[0, 0, pl.ds(x, 1)] = p[0:1]
        sy[0, 1, pl.ds(x, 1)] = p[cy - 1 : cy]

    for d in range(2):
        go(0, d, sy.at[0, d], ry.at[0, d ^ 1])

    loads[1].wait()
    for p in range(7):
        tile[p : p + 1, 0:blocks] = matrix_v[p, 0]
        tile[p : p + 1, 64 : 64 + blocks] = matrix_v[p + 7, 0]

    def gather_copy(ref, which, target):
        return pltpu.make_async_remote_copy(
            src_ref=ref[0], dst_ref=ref[1],
            send_sem=gsend_sem.at[which], recv_sem=grecv_sem.at[which],
            device_id=target, device_id_type=MESH,
        )

    tile_rows = gm.at[pl.ds(pl.multiple_of((gy * ngx + gx) * 8, 8), 8)]
    line_rows = gm.at[pl.ds(pl.multiple_of(gy * ngx * 8, 8), ngx * 8)]
    matrix_x = ((tile, tile_rows), 0, gm.at[pl.ds(0, (ngx - 1) * 8)])
    matrix_y = ((line_rows, line_rows), 1, gm.at[pl.ds(0, (ngy - 1) * ngx * 8)])
    sums_x = ((row, gr.at[gy, gx]), 2, gr.at[0, pl.ds(0, ngx - 1)])
    sums_y = ((gr.at[gy], gr.at[gy]), 3, gr.at[pl.ds(0, ngy - 1)])

    def start_all(plan, targets):
        for t in targets:
            gather_copy(plan[0], plan[1], t).start()

    def whole(plan):
        return gather_copy((plan[2], plan[2]), plan[1], along_y[0])

    loads[4].wait()
    loads[5].wait()

    @pl.loop(0, cx)
    def _(x):
        w = weight_v[x]
        sy[3, 0, pl.ds(x, 1)] = w[0:1]
        sy[3, 1, pl.ds(x, 1)] = w[cy - 1 : cy]
        m = map_v[x]
        sym[0, pl.ds(x, 1)] = m[0:1]
        sym[1, pl.ds(x, 1)] = m[cy - 1 : cy]

    loads[2].wait()
    loads[3].wait()

    for d in range(4):
        wait_halo(0, d, ry.at[0, d] if d < 2 else px.at[d - 2])

    for d in range(2):
        go(3, d, sy.at[3, d], ry.at[3, d ^ 1])
        go(4, d, sym.at[d], rym.at[d ^ 1])
        go(3, 2 + d, weight_h.at[(cx - 1) * d], wx.at[d ^ 1])
        go(4, 2 + d, map_h.at[(cx - 1) * d], mx.at[d ^ 1])

    def to_rows(buffer, stage):
        @pl.loop(0, cx)
        def _(x):
            buffer[x + 1, 15:16] = ry[stage, 0, pl.ds(x, 1)]
            buffer[x + 1, cy : cy + 1] = ry[stage, 1, pl.ds(x, 1)]

    pad_p[0, 0:cy] = px[0]
    pad_p[cx + 1, 0:cy] = px[1]
    to_rows(pad_p, 0)

    tx[0] = harmonic(pad_p[0], pad_p[1])
    lane = lax.broadcasted_iota(jnp.int32, (16, nz), 1)

    @pl.loop(0, cx)
    def _(x):
        p = pad_p[x + 1]
        up = harmonic(p, pad_p[x + 2])
        tx[x + 1] = up
        yp = harmonic(p, pltpu.roll(p, 15, 0))
        ym = pltpu.roll(yp, 1, 0)
        zp = jnp.where(lane == nz - 1, 0.0, harmonic(p, pltpu.roll(p, nz - 1, 1)))
        zm = pltpu.roll(zp, 1, 1)
        typ[x] = yp[0:cy]
        tym[x] = ym[0:cy]
        tzp[x] = zp[0:cy]
        tzm[x] = zm[0:cy]
        total = storage_v[x] + (up + tx[x] + yp + ym + zp + zm)[0:cy]
        inverse = 1.0 / total
        diag[x] = total
        inv[x] = inverse
        first = OMEGA * source_v[x] * inverse
        v1[x + 1, 0:cy] = first
        sy[1, 0, pl.ds(x, 1)] = first[0:1]
        sy[1, 1, pl.ds(x, 1)] = first[cy - 1 : cy]

    def field_halo(stage, v):
        for d in range(2):
            go(stage, d, sy.at[stage, d], ry.at[stage, d ^ 1])
        for d in range(2):
            sx[stage - 1, d, 0:cy] = v[1 + (cx - 1) * d, 0:cy]
            go(stage, 2 + d, sx.at[stage - 1, d], v.at[(cx + 1) * (1 - d)])

    def field_wait(stage, v):
        for d in range(4):
            wait_halo(stage, d, ry.at[stage, d] if d < 2 else v.at[(cx + 1) * (d - 2)])

    def operate(v, x):
        c = v[x + 1]
        total = tx[x + 1, 0:cy] * v[x + 2, 0:cy] + tx[x, 0:cy] * v[x, 0:cy]
        total += typ[x] * pltpu.roll(c, 15, 0)[0:cy] + tym[x] * pltpu.roll(c, 1, 0)[0:cy]
        total += tzp[x] * pltpu.roll(c, nz - 1, 1)[0:cy] + tzm[x] * pltpu.roll(c, 1, 1)[0:cy]
        return c[0:cy], diag[x] * c[0:cy] - total

    field_halo(1, v1)

    start_all(matrix_x, along_x)
    tile_rows[...] = tile[...]

    field_wait(1, v1)
    to_rows(v1, 1)

    @pl.loop(0, cx)
    def _(x):
        c, image = operate(v1, x)
        second = c + OMEGA * (source_v[x] - image) * inv[x]
        v2[x + 1, 0:cy] = second
        sy[2, 0, pl.ds(x, 1)] = second[0:1]
        sy[2, 1, pl.ds(x, 1)] = second[cy - 1 : cy]

    field_halo(2, v2)

    whole(matrix_x).wait_recv()
    start_all(matrix_y, along_y)

    field_wait(2, v2)
    to_rows(v2, 2)

    zline = lax.broadcasted_iota(jnp.int32, (cy, nz), 1)

    def is_here(cell_map):
        return zline - block * cell_map < block


    def gather(x, carry):
        same, before = carry
        c, image = operate(v2, x)
        value = weight_v[x] * (source_v[x] - image)
        here = is_here(map_v[x])
        return same + jnp.where(here, value, 0.0), before + jnp.where(here, 0.0, value)

    zero = jnp.zeros((cy, nz), F32)
    same, before = lax.fori_loop(0, cx, gather, (zero, zero))
    same = jnp.broadcast_to(jnp.sum(same, axis=0, keepdims=True), (16, nz))
    before = jnp.broadcast_to(jnp.sum(before, axis=0, keepdims=True), (16, nz))
    high, middle, low = pieces(same + pltpu.roll(before, nz - 1, 1))
    rows = lax.broadcasted_iota(jnp.int32, (16, nz), 0)
    stacked = jnp.where(rows == 0, high, jnp.where(rows == 1, middle, jnp.where(rows == 2, low, 0.0)))
    sums = jnp.dot(stacked.astype(jnp.bfloat16), ind[...], preferred_element_type=F32)
    mine = jnp.sum(sums, axis=0, keepdims=True)
    row[...] = mine

    start_all(sums_x, along_x)
    gr[gy, gx] = mine
    whole(sums_x).wait_recv()
    start_all(sums_y, along_y)

    whole(matrix_y).wait_recv()
    lower = lax.broadcasted_iota(jnp.int32, (ngy, 128), 1) < 64
    for p in range(7):
        for g in range(ngx):
            both = gm[pl.ds(g * 8 + p, ngy, stride=ngx * 8), :]
            coef[p, g] = jnp.where(lower, both, 0.0)
            coef[p + 7, g] = jnp.where(lower, pltpu.roll(both, 64, 1), 0.0)

    def moved(plane, dy, dz):
        if dz:
            plane = pltpu.roll(plane, dz % 128, 1)
        if dy:
            plane = pltpu.roll(plane, dy % ngy, 0)
        return plane

    for o in range(13):
        dx, dy, dz = o // 9 - 1, o // 3 % 3 - 1, o % 3 - 1
        for g in range(ngx):
            coef[26 - o, g] = moved(coef[o, (g - dx) % ngx], dy, dz)

    whole(sums_y).wait_recv()
    for g in range(ngx):
        for h in range(ngy):
            field[g, h : h + 1] = gr[h, g]

    def apply(u):
        result = [None] * ngx
        for dy in (-1, 0, 1):
            for dz in (-1, 0, 1):
                shifted = [moved(plane, -dy, -dz) for plane in u]
                for dx in (-1, 0, 1):
                    o = 9 * (dx + 1) + 3 * (dy + 1) + dz + 1
                    for g in range(ngx):
                        if 0 <= g + dx < ngx:
                            term = coef[o, g] * shifted[g + dx]
                            result[g] = term if result[g] is None else result[g] + term
        return result

    def inner(a, b):
        total = a[0] * b[0]
        for g in range(1, ngx):
            total = total + a[g] * b[g]
        return jnp.sum(jnp.sum(total, axis=0, keepdims=True), axis=1, keepdims=True)

    residual = [field[g] for g in range(ngx)]
    direction = residual
    answer = [jnp.zeros((ngy, 128), F32)] * ngx
    norm = inner(residual, residual)
    for iteration in range(ITERS):
        applied = apply(direction)
        step = norm / inner(direction, applied)
        answer = [a + step * b for a, b in zip(answer, direction)]
        if iteration + 1 < ITERS:
            residual = [a - step * b for a, b in zip(residual, applied)]
            following = inner(residual, residual)
            ratio = following / norm
            direction = [a + ratio * b for a, b in zip(residual, direction)]
            norm = following
    for g in range(ngx):
        field[g] = answer[g]

    west, east = jnp.maximum(gx - 1, 0), jnp.minimum(gx + 1, ngx - 1)
    south, north = jnp.maximum(gy - 1, 0), jnp.minimum(gy + 1, ngy - 1)
    picks = ((gx, gy), (gx, south), (gx, north), (west, gy), (east, gy))
    rows = lax.broadcasted_iota(jnp.int32, (16, 128), 0)
    stacked = jnp.zeros((16, 128), F32)
    for i, (a, b) in enumerate(picks):
        value = jnp.broadcast_to(field[a, pl.ds(b, 1)], (16, 128))
        for j, piece in enumerate(pieces(value)):
            stacked = jnp.where(rows == 3 * i + j, piece, stacked)
    spread[...] = jnp.dot(stacked.astype(jnp.bfloat16), indt[...], preferred_element_type=F32)

    def by_block(i):
        value = spread[3 * i : 3 * i + 1] + spread[3 * i + 1 : 3 * i + 2] + spread[3 * i + 2 : 3 * i + 3]
        value = jnp.broadcast_to(value, (16, nz))
        return value[0:cy], pltpu.roll(value, 1, 1)[0:cy]

    for d in range(4):
        wait_halo(3, d, ry.at[3, d] if d < 2 else wx.at[d - 2])
        wait_halo(4, d, rym.at[d] if d < 2 else mx.at[d - 2])

    for d in range(2):
        now, prior = by_block(1 + d)
        ry[2, d] = ry[2, d] + ry[3, d] * jnp.where(is_here(rym[d]), now, prior)
        now, prior = by_block(3 + d)
        at = d * (cx + 1)
        v1[at, 0:cy] = v2[at, 0:cy] + wx[d] * jnp.where(is_here(mx[d]), now, prior)

    now, prior = by_block(0)

    @pl.loop(0, cx)
    def _(x):
        value = v2[x + 1, 0:cy] + weight_v[x] * jnp.where(is_here(map_v[x]), now, prior)
        pressure_v[x] = value

    out = pltpu.make_async_copy(pressure_v, pressure_h, local_sem.at[6])
    out.start()
    for item in sent:
        wait_sent(*item)

    @pl.loop(0, cx)
    def _(x):
        v1[x + 1, 0:cy] = pressure_v[x]

    to_rows(v1, 2)

    @pl.loop(0, cx)
    def _(x):
        c, image = operate(v1, x)
        final_v[x] = source_v[x] - image

    out2 = pltpu.make_async_copy(final_v, final_h, local_sem.at[7])
    out2.start()
    for plan in (matrix_x, matrix_y, sums_x, sums_y):
        whole(plan).wait_send()
    out.wait()
    out2.wait()


def solution(mesh):
    ngx, ngy = mesh.shape["gx"], mesh.shape["gy"]

    def shards(perm, storage, source, weight, block_map, matrix):
        cx, cy, nz = perm.shape
        block = nz // matrix.shape[-1]
        n = ngx * ngy
        brick = pltpu.VMEM((cx, cy, nz), F32)
        padded = pltpu.VMEM((cx + 2, 16, nz), F32)
        face = pltpu.VMEM((2, cy, nz), F32)
        shape = jax.ShapeDtypeStruct(perm.shape, F32)
        return pl.pallas_call(
            functools.partial(kernel, ngx, ngy, block),
            out_shape=(shape, shape),
            in_specs=[pl.BlockSpec(memory_space=pltpu.HBM)] * 6,
            out_specs=[pl.BlockSpec(memory_space=pltpu.HBM)] * 2,
            scratch_shapes=[
                brick, brick, brick, brick, pltpu.VMEM((cx, cy, nz), jnp.int32),
                pltpu.VMEM(matrix.shape, F32),
                padded, padded, padded, pltpu.VMEM((cx + 1, 16, nz), F32),
                brick, brick, brick, brick, brick, brick,
                pltpu.VMEM((4, 2, cx, nz), F32), pltpu.VMEM((4, 2, cx, nz), F32),
                pltpu.VMEM((2, 2, 16, nz), F32),
                pltpu.VMEM((2, cx, nz), jnp.int32), pltpu.VMEM((2, cx, nz), jnp.int32),
                face, face, pltpu.VMEM((2, cy, nz), jnp.int32),
                pltpu.VMEM((8, 128), F32), pltpu.VMEM((n * 8, 128), F32),
                pltpu.VMEM((27, ngx, ngy, 128), F32),
                pltpu.VMEM((1, 128), F32), pltpu.VMEM((ngy, ngx, 1, 128), F32),
                pltpu.VMEM((ngx, ngy, 128), F32), pltpu.VMEM((16, nz), F32),
                pltpu.VMEM((nz, 128), jnp.bfloat16), pltpu.VMEM((128, nz), jnp.bfloat16),
                brick, brick,
                pltpu.SemaphoreType.DMA((8,)),
                pltpu.SemaphoreType.DMA((20,)), pltpu.SemaphoreType.DMA((20,)),
                pltpu.SemaphoreType.DMA((4,)), pltpu.SemaphoreType.DMA((4,)),
            ],
            compiler_params=pltpu.CompilerParams(
                collective_id=0, has_side_effects=True, vmem_limit_bytes=63 << 20
            ),
        )(perm, storage, source, weight, block_map, matrix)

    fine = P("gx", "gy", None)
    return jax.shard_map(
        shards,
        mesh=mesh,
        in_specs=(fine,) * 5 + (P(None, "gx", "gy", None),),
        out_specs=(fine, fine),
        check_vma=False,
    )
```

```python
import functools

import jax
import jax.numpy as jnp
from jax import lax
from jax.experimental import pallas as pl
from jax.experimental.pallas import tpu as pltpu
from jax.sharding import PartitionSpec as P

ITERS = 6
OMEGA = 0.8
MESH = pl.DeviceIdType.MESH
F32 = jnp.float32


def harmonic(a, b):
    return 2.0 * a * b / (a + b)


def pieces(value):
    high = value.astype(jnp.bfloat16).astype(F32)
    rest = value - high
    middle = rest.astype(jnp.bfloat16).astype(F32)
    return high, middle, rest - middle


def kernel(
    ngx, ngy, block,
    perm_h, storage_h, source_h, weight_h, map_h, matrix_h,
    pressure_h, final_h,
    perm_v, storage_v, source_v, weight_v, map_v, matrix_v,
    pad_p, v1, v2, tx, typ, tym, tzp, tzm, diag, inv,
    sy, ry, sx, sym, rym, px, wx, mx,
    tile, gm, coef, row, gr, field, spread, ind, indt,
    pressure_v, final_v,
    local_sem, send_sem, recv_sem, gsend_sem, grecv_sem,
):
    cx, cy, nz = perm_v.shape
    half = cx // 2
    blocks = matrix_v.shape[-1]
    gx, gy = lax.axis_index("gx"), lax.axis_index("gy")
    has = (gy > 0, gy < ngy - 1, gx > 0, gx < ngx - 1)
    near = ((gx, gy - 1), (gx, gy + 1), (gx - 1, gy), (gx + 1, gy))

    loads = [
        pltpu.make_async_copy(src, dst, local_sem.at[i])
        for i, (src, dst) in enumerate((
            (perm_h, perm_v), (matrix_h, matrix_v), (source_h, source_v),
            (storage_h, storage_v), (weight_h, weight_v), (map_h, map_v),
        ))
    ]
    for load in loads:
        load.start()

    def around(at, step, size):
        moved_on = at + step
        return jnp.where(moved_on >= size, moved_on - size, moved_on)

    along_x = [(around(gx, a, ngx), gy) for a in range(1, ngx)]
    along_y = [(gx, around(gy, b, ngy)) for b in range(1, ngy)]

    barrier = pltpu.get_barrier_semaphore()

    for t in along_x + along_y:
        pl.semaphore_signal(barrier, inc=1, device_id=t, device_id_type=MESH)

    for d in range(2):
        @pl.when(jnp.logical_not(has[d]))
        def _():
            for s in range(4):
                ry[s, d] = jnp.zeros(ry.shape[2:], F32)
            rym[d] = jnp.zeros(rym.shape[1:], jnp.int32)

        @pl.when(jnp.logical_not(has[2 + d]))
        def _():
            px[d] = jnp.zeros(px.shape[1:], F32)
            wx[d] = jnp.zeros(wx.shape[1:], F32)
            mx[d] = jnp.zeros(mx.shape[1:], jnp.int32)
            for v in (v1, v2):
                v[d * (cx + 1)] = jnp.zeros(v.shape[1:], F32)

    def inside(shape, z_dim):
        z = lax.broadcasted_iota(jnp.int32, shape, z_dim)
        offset = z - block * lax.broadcasted_iota(jnp.int32, shape, 1 - z_dim)
        return ((offset >= 0) & (offset < block)).astype(F32).astype(jnp.bfloat16)

    ind[...] = inside((nz, 128), 0)
    indt[...] = inside((128, nz), 1)
    pad_p[...] = jnp.ones(pad_p.shape, F32)
    tile[...] = jnp.zeros(tile.shape, F32)
    sx[...] = jnp.zeros(sx.shape, F32)

    pl.semaphore_wait(barrier, ngx + ngy - 2)

    def mark(stage, d, part):
        return 20 + stage * 2 + d if part else stage * 4 + d

    def halo(stage, d, src, dst, part=0):
        return pltpu.make_async_remote_copy(
            src_ref=src, dst_ref=dst,
            send_sem=send_sem.at[mark(stage, d, part)],
            recv_sem=recv_sem.at[mark(stage, d ^ 1, part)],
            device_id=near[d], device_id_type=MESH,
        )

    def send(stage, d, src, dst, part=0):
        @pl.when(has[d])
        def _():
            halo(stage, d, src, dst, part).start()

    def wait_sent(stage, d, src, dst, part=0):
        @pl.when(has[d])
        def _():
            halo(stage, d, src, dst, part).wait_send()

    def wait_halo(stage, d, dst, part=0):
        @pl.when(has[d])
        def _():
            pltpu.make_async_remote_copy(
                src_ref=dst, dst_ref=dst,
                send_sem=send_sem.at[mark(stage, d, part)],
                recv_sem=recv_sem.at[mark(stage, d, part)],
                device_id=near[d], device_id_type=MESH,
            ).wait_recv()

    sent = []

    def go(stage, d, src, dst, part=0):
        send(stage, d, src, dst, part)
        sent.append((stage, d, src, dst, part))

    for d in range(2):
        go(0, 2 + d, perm_h.at[(cx - 1) * d], px.at[d ^ 1])
    loads[0].wait()

    @pl.loop(0, cx)
    def _(x):
        p = perm_v[x]
        pad_p[x + 1, 0:cy] = p
        sy[0, 0, x // half, pl.ds(x % half, 1)] = p[0:1]
        sy[0, 1, x // half, pl.ds(x % half, 1)] = p[cy - 1 : cy]

    for d in range(2):
        go(0, d, sy.at[0, d], ry.at[0, d ^ 1])

    loads[1].wait()
    for p in range(7):
        tile[p : p + 1, 0:blocks] = matrix_v[p, 0]
        tile[p : p + 1, 64 : 64 + blocks] = matrix_v[p + 7, 0]

    def gather_copy(ref, which, target):
        return pltpu.make_async_remote_copy(
            src_ref=ref[0], dst_ref=ref[1],
            send_sem=gsend_sem.at[which], recv_sem=grecv_sem.at[which],
            device_id=target, device_id_type=MESH,
        )

    tile_rows = gm.at[pl.ds(pl.multiple_of((gy * ngx + gx) * 8, 8), 8)]
    line_rows = gm.at[pl.ds(pl.multiple_of(gy * ngx * 8, 8), ngx * 8)]
    matrix_x = ((tile, tile_rows), 0, gm.at[pl.ds(0, (ngx - 1) * 8)])
    matrix_y = ((line_rows, line_rows), 1, gm.at[pl.ds(0, (ngy - 1) * ngx * 8)])
    sums_x = ((row, gr.at[gy, gx]), 2, gr.at[0, pl.ds(0, ngx - 1)])
    sums_y = ((gr.at[gy], gr.at[gy]), 3, gr.at[pl.ds(0, ngy - 1)])

    def start_all(plan, targets):
        for t in targets:
            gather_copy(plan[0], plan[1], t).start()

    def whole(plan):
        return gather_copy((plan[2], plan[2]), plan[1], along_y[0])

    loads[4].wait()
    loads[5].wait()

    @pl.loop(0, cx)
    def _(x):
        w = weight_v[x]
        sy[3, 0, x // half, pl.ds(x % half, 1)] = w[0:1]
        sy[3, 1, x // half, pl.ds(x % half, 1)] = w[cy - 1 : cy]
        m = map_v[x]
        sym[0, x // half, pl.ds(x % half, 1)] = m[0:1]
        sym[1, x // half, pl.ds(x % half, 1)] = m[cy - 1 : cy]

    loads[2].wait()
    loads[3].wait()

    for d in range(4):
        wait_halo(0, d, ry.at[0, d] if d < 2 else px.at[d - 2])

    for d in range(2):
        go(3, d, sy.at[3, d], ry.at[3, d ^ 1])
        go(4, d, sym.at[d], rym.at[d ^ 1])
        go(3, 2 + d, weight_h.at[(cx - 1) * d], wx.at[d ^ 1])
        go(4, 2 + d, map_h.at[(cx - 1) * d], mx.at[d ^ 1])

    def to_rows(buffer, stage, parts=(0, 1)):
        for h in parts:
            for i in range(half):
                x = h * half + i + 1
                buffer[x, 15:16] = ry[stage, 0, h, i : i + 1]
                buffer[x, cy : cy + 1] = ry[stage, 1, h, i : i + 1]

    pad_p[0, 0:cy] = px[0]
    pad_p[cx + 1, 0:cy] = px[1]
    to_rows(pad_p, 0)

    tx[0] = harmonic(pad_p[0], pad_p[1])
    lane = lax.broadcasted_iota(jnp.int32, (16, nz), 1)

    def faces(x, i, h):
        p = pad_p[x + 1]
        up = harmonic(p, pad_p[x + 2])
        tx[x + 1] = up
        yp = harmonic(p, pltpu.roll(p, 15, 0))
        ym = pltpu.roll(yp, 1, 0)
        zp = jnp.where(lane == nz - 1, 0.0, harmonic(p, pltpu.roll(p, nz - 1, 1)))
        zm = pltpu.roll(zp, 1, 1)
        typ[x] = yp[0:cy]
        tym[x] = ym[0:cy]
        tzp[x] = zp[0:cy]
        tzm[x] = zm[0:cy]
        total = storage_v[x] + (up + tx[x] + yp + ym + zp + zm)[0:cy]
        inverse = 1.0 / total
        diag[x] = total
        inv[x] = inverse
        first = OMEGA * source_v[x] * inverse
        v1[x + 1, 0:cy] = first
        sy[1, 0, h, pl.ds(i, 1)] = first[0:1]
        sy[1, 1, h, pl.ds(i, 1)] = first[cy - 1 : cy]

    def halves(act, stage, v, before=None):
        for h in range(2):
            if before is not None:
                before(h)

            @pl.loop(0, half)
            def _(i):
                act(h * half + i, i, h)

            for d in range(2):
                go(stage, d, sy.at[stage, d, h], ry.at[stage, d ^ 1, h], h)
            sx[stage - 1, h, 0:cy] = v[1 + (cx - 1) * h, 0:cy]
            go(stage, 2 + h, sx.at[stage - 1, h], v.at[(cx + 1) * (1 - h)])

    def field_wait(stage, v, h):
        for d in range(2):
            wait_halo(stage, d, ry.at[stage, d, h], h)
        wait_halo(stage, 2 + h, v.at[(cx + 1) * h])
        to_rows(v, stage, (h,))

    def operate(v, x):
        c = v[x + 1]
        total = tx[x + 1, 0:cy] * v[x + 2, 0:cy] + tx[x, 0:cy] * v[x, 0:cy]
        total += typ[x] * pltpu.roll(c, 15, 0)[0:cy] + tym[x] * pltpu.roll(c, 1, 0)[0:cy]
        total += tzp[x] * pltpu.roll(c, nz - 1, 1)[0:cy] + tzm[x] * pltpu.roll(c, 1, 1)[0:cy]
        return c[0:cy], diag[x] * c[0:cy] - total

    halves(faces, 1, v1)

    start_all(matrix_x, along_x)
    tile_rows[...] = tile[...]

    def smooth(x, i, h):
        c, image = operate(v1, x)
        second = c + OMEGA * (source_v[x] - image) * inv[x]
        v2[x + 1, 0:cy] = second
        sy[2, 0, h, pl.ds(i, 1)] = second[0:1]
        sy[2, 1, h, pl.ds(i, 1)] = second[cy - 1 : cy]

    halves(smooth, 2, v2, lambda h: field_wait(1, v1, h))

    whole(matrix_x).wait_recv()
    start_all(matrix_y, along_y)

    zline = lax.broadcasted_iota(jnp.int32, (cy, nz), 1)

    def is_here(cell_map):
        return zline - block * cell_map < block


    def gather(x, carry):
        same, before = carry
        c, image = operate(v2, x)
        value = weight_v[x] * (source_v[x] - image)
        here = is_here(map_v[x])
        return same + jnp.where(here, value, 0.0), before + jnp.where(here, 0.0, value)

    zero = jnp.zeros((cy, nz), F32)
    field_wait(2, v2, 0)
    carry = lax.fori_loop(0, half, gather, (zero, zero))
    field_wait(2, v2, 1)
    same, before = lax.fori_loop(half, cx, gather, carry)
    same = jnp.broadcast_to(jnp.sum(same, axis=0, keepdims=True), (16, nz))
    before = jnp.broadcast_to(jnp.sum(before, axis=0, keepdims=True), (16, nz))
    high, middle, low = pieces(same + pltpu.roll(before, nz - 1, 1))
    rows = lax.broadcasted_iota(jnp.int32, (16, nz), 0)
    stacked = jnp.where(rows == 0, high, jnp.where(rows == 1, middle, jnp.where(rows == 2, low, 0.0)))
    sums = jnp.dot(stacked.astype(jnp.bfloat16), ind[...], preferred_element_type=F32)
    mine = jnp.sum(sums, axis=0, keepdims=True)
    row[...] = mine

    start_all(sums_x, along_x)
    gr[gy, gx] = mine
    whole(sums_x).wait_recv()
    start_all(sums_y, along_y)

    whole(matrix_y).wait_recv()
    lower = lax.broadcasted_iota(jnp.int32, (ngy, 128), 1) < 64
    for p in range(7):
        for g in range(ngx):
            both = gm[pl.ds(g * 8 + p, ngy, stride=ngx * 8), :]
            coef[p, g] = jnp.where(lower, both, 0.0)
            coef[p + 7, g] = jnp.where(lower, pltpu.roll(both, 64, 1), 0.0)

    def moved(plane, dy, dz):
        if dz:
            plane = pltpu.roll(plane, dz % 128, 1)
        if dy:
            plane = pltpu.roll(plane, dy % ngy, 0)
        return plane

    for o in range(13):
        dx, dy, dz = o // 9 - 1, o // 3 % 3 - 1, o % 3 - 1
        for g in range(ngx):
            coef[26 - o, g] = moved(coef[o, (g - dx) % ngx], dy, dz)

    whole(sums_y).wait_recv()
    for g in range(ngx):
        for h in range(ngy):
            field[g, h : h + 1] = gr[h, g]

    def apply(u):
        result = [None] * ngx
        for dy in (-1, 0, 1):
            for dz in (-1, 0, 1):
                shifted = [moved(plane, -dy, -dz) for plane in u]
                for dx in (-1, 0, 1):
                    o = 9 * (dx + 1) + 3 * (dy + 1) + dz + 1
                    for g in range(ngx):
                        if 0 <= g + dx < ngx:
                            term = coef[o, g] * shifted[g + dx]
                            result[g] = term if result[g] is None else result[g] + term
        return result

    def inner(a, b):
        total = a[0] * b[0]
        for g in range(1, ngx):
            total = total + a[g] * b[g]
        return jnp.sum(jnp.sum(total, axis=0, keepdims=True), axis=1, keepdims=True)

    residual = [field[g] for g in range(ngx)]
    direction = residual
    answer = [jnp.zeros((ngy, 128), F32)] * ngx
    norm = inner(residual, residual)
    for iteration in range(ITERS):
        applied = apply(direction)
        step = norm / inner(direction, applied)
        answer = [a + step * b for a, b in zip(answer, direction)]
        if iteration + 1 < ITERS:
            residual = [a - step * b for a, b in zip(residual, applied)]
            following = inner(residual, residual)
            ratio = following / norm
            direction = [a + ratio * b for a, b in zip(residual, direction)]
            norm = following
    for g in range(ngx):
        field[g] = answer[g]

    west, east = jnp.maximum(gx - 1, 0), jnp.minimum(gx + 1, ngx - 1)
    south, north = jnp.maximum(gy - 1, 0), jnp.minimum(gy + 1, ngy - 1)
    picks = ((gx, gy), (gx, south), (gx, north), (west, gy), (east, gy))
    rows = lax.broadcasted_iota(jnp.int32, (16, 128), 0)
    stacked = jnp.zeros((16, 128), F32)
    for i, (a, b) in enumerate(picks):
        value = jnp.broadcast_to(field[a, pl.ds(b, 1)], (16, 128))
        for j, piece in enumerate(pieces(value)):
            stacked = jnp.where(rows == 3 * i + j, piece, stacked)
    spread[...] = jnp.dot(stacked.astype(jnp.bfloat16), indt[...], preferred_element_type=F32)

    def by_block(i):
        value = spread[3 * i : 3 * i + 1] + spread[3 * i + 1 : 3 * i + 2] + spread[3 * i + 2 : 3 * i + 3]
        value = jnp.broadcast_to(value, (16, nz))
        return value[0:cy], pltpu.roll(value, 1, 1)[0:cy]

    for d in range(4):
        wait_halo(3, d, ry.at[3, d] if d < 2 else wx.at[d - 2])
        wait_halo(4, d, rym.at[d] if d < 2 else mx.at[d - 2])

    for d in range(2):
        now, prior = by_block(1 + d)
        for h in range(2):
            choice = jnp.where(zline[0:half] - block * rym[d, h] < block, now[0:half], prior[0:half])
            ry[2, d, h] = ry[2, d, h] + ry[3, d, h] * choice
        now, prior = by_block(3 + d)
        at = d * (cx + 1)
        v1[at, 0:cy] = v2[at, 0:cy] + wx[d] * jnp.where(is_here(mx[d]), now, prior)

    now, prior = by_block(0)

    @pl.loop(0, cx)
    def _(x):
        value = v2[x + 1, 0:cy] + weight_v[x] * jnp.where(is_here(map_v[x]), now, prior)
        pressure_v[x] = value

    out = pltpu.make_async_copy(pressure_v, pressure_h, local_sem.at[6])
    out.start()
    for item in sent:
        wait_sent(*item)

    @pl.loop(0, cx)
    def _(x):
        v1[x + 1, 0:cy] = pressure_v[x]

    to_rows(v1, 2)

    @pl.loop(0, cx)
    def _(x):
        c, image = operate(v1, x)
        final_v[x] = source_v[x] - image

    out2 = pltpu.make_async_copy(final_v, final_h, local_sem.at[7])
    out2.start()
    for plan in (matrix_x, matrix_y, sums_x, sums_y):
        whole(plan).wait_send()
    out.wait()
    out2.wait()


def solution(mesh):
    ngx, ngy = mesh.shape["gx"], mesh.shape["gy"]

    def shards(perm, storage, source, weight, block_map, matrix):
        cx, cy, nz = perm.shape
        block = nz // matrix.shape[-1]
        n = ngx * ngy
        brick = pltpu.VMEM((cx, cy, nz), F32)
        padded = pltpu.VMEM((cx + 2, 16, nz), F32)
        face = pltpu.VMEM((2, cy, nz), F32)
        shape = jax.ShapeDtypeStruct(perm.shape, F32)
        return pl.pallas_call(
            functools.partial(kernel, ngx, ngy, block),
            out_shape=(shape, shape),
            in_specs=[pl.BlockSpec(memory_space=pltpu.HBM)] * 6,
            out_specs=[pl.BlockSpec(memory_space=pltpu.HBM)] * 2,
            scratch_shapes=[
                brick, brick, brick, brick, pltpu.VMEM((cx, cy, nz), jnp.int32),
                pltpu.VMEM(matrix.shape, F32),
                padded, padded, padded, pltpu.VMEM((cx + 1, 16, nz), F32),
                brick, brick, brick, brick, brick, brick,
                pltpu.VMEM((4, 2, 2, cx // 2, nz), F32), pltpu.VMEM((4, 2, 2, cx // 2, nz), F32),
                pltpu.VMEM((2, 2, 16, nz), F32),
                pltpu.VMEM((2, 2, cx // 2, nz), jnp.int32), pltpu.VMEM((2, 2, cx // 2, nz), jnp.int32),
                face, face, pltpu.VMEM((2, cy, nz), jnp.int32),
                pltpu.VMEM((8, 128), F32), pltpu.VMEM((n * 8, 128), F32),
                pltpu.VMEM((27, ngx, ngy, 128), F32),
                pltpu.VMEM((1, 128), F32), pltpu.VMEM((ngy, ngx, 1, 128), F32),
                pltpu.VMEM((ngx, ngy, 128), F32), pltpu.VMEM((16, nz), F32),
                pltpu.VMEM((nz, 128), jnp.bfloat16), pltpu.VMEM((128, nz), jnp.bfloat16),
                brick, brick,
                pltpu.SemaphoreType.DMA((8,)),
                pltpu.SemaphoreType.DMA((30,)), pltpu.SemaphoreType.DMA((30,)),
                pltpu.SemaphoreType.DMA((4,)), pltpu.SemaphoreType.DMA((4,)),
            ],
            compiler_params=pltpu.CompilerParams(
                collective_id=0, has_side_effects=True, vmem_limit_bytes=63 << 20
            ),
        )(perm, storage, source, weight, block_map, matrix)

    fine = P("gx", "gy", None)
    return jax.shard_map(
        shards,
        mesh=mesh,
        in_specs=(fine,) * 5 + (P(None, "gx", "gy", None),),
        out_specs=(fine, fine),
        check_vma=False,
    )
```
